128 devices in a mesh: dp: 8 (over x, y_lo), fsdp: 16 (over y_hi, z, core).
Axes of the slice: x: 4, y: 4 (y_hi: 2, y_lo: 2; y = y_hi * 2 + y_lo), z: 4, core: 2. Of those that a mesh axis runs over, the one named last changes fastest.
Arguments:
- tokens: bfloat16 [16384, 3072], P(('dp', 'fsdp')), may hold values from -6 to 6
- hess_tokens: bfloat16 [4096, 3072], P(('dp', 'fsdp')), may hold values from -6 to 6
- upstream: bfloat16 [16384, 12288], P('dp', 'fsdp'), may hold values from -5 to 5
- hess_upstream: bfloat16 [4096, 12288], P('dp', 'fsdp'), may hold values from -0.75 to 0.75
- weight: bfloat16 [3072, 12288], P(None, 'fsdp'), may hold values from -0.109375 to 0.109375
- probes: bfloat16 [3072, 12288], P('dp', 'fsdp'), may hold values from -6 to 6
- momentum: float32 [3072, 12288], P('dp', 'fsdp'), may hold values from -0.3 to 0.3
- curvature: float32 [3072, 12288], P('dp', 'fsdp'), may hold values from 0.1 to 10
Outputs:
- new_weight: bfloat16 [3072, 12288], P('dp', 'fsdp')
- new_momentum: float32 [3072, 12288], P('dp', 'fsdp')
- new_curvature: float32 [3072, 12288], P('dp', 'fsdp')
The draws below stay inside these ranges and needn't reach their ends.
All inputs are finite; a program needn't handle non-finite values.
Results may differ from the reference program's by a relative error of at most 0.015.
Values may be sent and summed in bfloat16 or wider, within the bound.
No kernel may reach another device: no remote copies, remote signals or barrier semaphores. Data moves between devices by JAX's collectives and lax.ppermute only.
A program may use at most 128 MiB of HBM per device.

```python
import math
import jax
import jax.numpy as jnp
from jax import lax

D = 3072
FF = 12288
TOK_DEV = 128
HESS_DEV = 32
TOKENS = 16384
HTOKENS = 4096
N_DP = 8
N_FSDP = 16


def steps_of(stream_key, shape, pieces, low, largest):
    gain = 1.0
    for axis_at, blocks in pieces:
        heights = jax.random.uniform(jax.random.fold_in(jax.random.fold_in(stream_key, 6), axis_at), (blocks,), jnp.float32, low / len(pieces), largest / len(pieces))
        gain = gain * jnp.repeat(jnp.exp(heights), shape[axis_at] // blocks).reshape((-1,) + (1,) * (len(shape) - 1 - axis_at))
    return gain


def normal_values(own_key, extent, scale, bound, split=(), kind=jnp.bfloat16):
    factor_of = steps_of(own_key, extent, split, -0.22, 0.18) if split else 1.0
    result = jax.random.normal(own_key, extent, jnp.float32) * scale * factor_of
    return jnp.minimum(jnp.maximum(result, -bound), bound).astype(kind)


def setup_inputs(seed: int = 0) -> dict:
    seeds = jax.random.split(jax.random.key(seed), 9)
    return {
        "tokens": normal_values(seeds[0], (TOKENS, D), 1.0, 6.0, ((0, 128),)),
        "hess_tokens": normal_values(seeds[1], (HTOKENS, D), 1.0, 6.0, ((0, 128),)),
        "upstream": normal_values(seeds[2], (TOKENS, FF), (4 * TOK_DEV ** -0.5), 5.0, ((0, 8), (1, 16))),
        "hess_upstream": normal_values(seeds[3], (HTOKENS, FF), (16 * HESS_DEV ** -0.5 * D ** -0.5), 0.75, ((0, 8), (1, 16))),
        "weight": normal_values(seeds[4], (D, FF), D ** -0.5, 0.109375, ((1, 16),)),
        "probes": normal_values(seeds[5], (D, FF), 1.0, 6.0, ((0, 8), (1, 16))),
        "momentum": normal_values(seeds[6], (D, FF), 0.05, 0.3, ((0, 8), (1, 16)), jnp.float32),
        "curvature": jnp.clip(jnp.exp(math.log(10.0) - 4.6051702 * jax.random.uniform(seeds[7], (D, FF), jnp.float32) ** steps_of(seeds[7], (D, FF), ((0, 8), (1, 16)), -0.2, 0.2)), 0.1, 10.0),
    }


SQRT_HALF = 1.0 / math.sqrt(2.0)
INV_ROOT_TAU = 1.0 / math.sqrt(2.0 * math.pi)
BETA_ONE = 0.965
BETA_TWO = 0.99
LEARN_RATE = 0.0006
WEIGHT_DECAY = 0.1
HESS_SCALE = 0.01
RATIO_FLOOR = 0.001

def gelu_slope(preact):
    normal_cdf = 0.5 * (1.0 + jax.scipy.special.erf(preact * SQRT_HALF))
    density = jnp.exp(-0.5 * preact * preact) * INV_ROOT_TAU
    return normal_cdf + preact * density

def gelu_bend(preact):
    density = jnp.exp(-0.5 * preact * preact) * INV_ROOT_TAU
    return density * (2.0 - preact * preact)

def rounded(value):
    narrow = lax.optimization_barrier(value.astype(jnp.bfloat16))
    return narrow.astype(jnp.float32)

def reference(tokens, hess_tokens, upstream, hess_upstream, weight, probes, momentum, curvature):
    group_rows = TOK_DEV * N_FSDP
    hess_rows = HESS_DEV * N_FSDP
    gradient = jnp.zeros((D, FF), jnp.float32)
    hessian_vec = jnp.zeros((D, FF), jnp.float32)
    for replica in range(N_DP):
        batch_rows = tokens[replica * group_rows:(replica + 1) * group_rows]
        signal = upstream[replica * group_rows:(replica + 1) * group_rows]
        preact = jnp.dot(batch_rows, weight, preferred_element_type=jnp.float32)
        slopes = (signal.astype(jnp.float32) * gelu_slope(preact)).astype(jnp.bfloat16)
        gradient = gradient + rounded(jnp.dot(batch_rows.T, slopes, preferred_element_type=jnp.float32))
        hess_block = hess_tokens[replica * hess_rows:(replica + 1) * hess_rows]
        hess_signal = hess_upstream[replica * hess_rows:(replica + 1) * hess_rows]
        hess_pre = jnp.dot(hess_block, weight, preferred_element_type=jnp.float32)
        tangent = jnp.dot(hess_block, probes, preferred_element_type=jnp.float32)
        curved = (hess_signal.astype(jnp.float32) * gelu_bend(hess_pre) * tangent).astype(jnp.bfloat16)
        hessian_vec = hessian_vec + rounded(jnp.dot(hess_block.T, curved, preferred_element_type=jnp.float32))
    new_curvature = BETA_TWO * curvature + (1.0 - BETA_TWO) * (probes.astype(jnp.float32) * hessian_vec)
    new_momentum = BETA_ONE * momentum + (1.0 - BETA_ONE) * gradient
    ratio = jnp.clip(new_momentum / jnp.maximum(HESS_SCALE * new_curvature, RATIO_FLOOR), -1.0, 1.0)
    new_weight = (weight.astype(jnp.float32) * (1.0 - LEARN_RATE * WEIGHT_DECAY) - LEARN_RATE * ratio).astype(jnp.bfloat16)
    return (new_weight, new_momentum, new_curvature)
```

```python
import math

import jax
import jax.numpy as jnp
from jax import lax
from jax.experimental import pallas as pl
from jax.experimental.pallas import tpu as pltpu
from jax.sharding import PartitionSpec as P

SQRT_HALF = 1.0 / math.sqrt(2.0)
INV_ROOT_TAU = 1.0 / math.sqrt(2.0 * math.pi)
BETA_ONE = 0.965
BETA_TWO = 0.99
LEARN_RATE = 0.0006
WEIGHT_DECAY = 0.1
HESS_SCALE = 0.01
RATIO_FLOOR = 0.001

D = 3072
COLS = 768
HALF = COLS // 2
ROWS = 384
PAIR = 2 * ROWS
TOK = 128
HESS = 32
VMEM = 48 << 20
AXES = ("dp", "fsdp")
BF16 = jnp.bfloat16
F32 = jnp.float32


def device_index(x, y, z, core):
    return (x * 2 + y % 2) * 16 + (y // 2) * 8 + z * 2 + core


def moves(step):
    pairs = []
    for x in range(4):
        for y in range(4):
            for z in range(4):
                for core in range(2):
                    if step == "y^":
                        to = (x, y ^ 1, z, core)
                    else:
                        to = ((x + step[0]) % 4, (y + step[1]) % 4, (z + step[2]) % 4, (core + step[3]) % 2)
                    pairs.append((device_index(x, y, z, core), device_index(*to)))
    return pairs


X_UP, X_DOWN = (1, 0, 0, 0), (3, 0, 0, 0)
Y_UP, Y_DOWN, Y_TWO = (0, 1, 0, 0), (0, 3, 0, 0), (0, 2, 0, 0)
Z_UP, Z_DOWN = (0, 0, 1, 0), (0, 0, 3, 0)
SWAP = (0, 0, 0, 1)
Y_PAIR = "y^"


def send(value, step):
    return lax.ppermute(value, AXES, moves(step))


def gelu_slope(preact):
    normal_cdf = 0.5 * (1.0 + lax.erf(preact * SQRT_HALF))
    density = jnp.exp(-0.5 * preact * preact) * INV_ROOT_TAU
    return normal_cdf + preact * density


def gelu_bend(preact):
    density = jnp.exp(-0.5 * preact * preact) * INV_ROOT_TAU
    return density * (2.0 - preact * preact)


def forward(pairs, weight, upstream, first):
    blocks = [b for pair in pairs for b in pair]
    n, width = len(blocks), 256

    def kernel(first_ref, *refs):
        tokens, w_ref, u_ref, out_ref = refs[:n], refs[n], refs[n + 1], refs[n + 2]
        for i in range(0, n, 2):
            rows = jnp.concatenate([tokens[i][...], tokens[i + 1][...]], 0)
            slope = gelu_slope(jnp.dot(rows, w_ref[...], preferred_element_type=F32))
            for j in range(2):
                at = pl.multiple_of(first_ref[i + j], TOK)
                signal = u_ref[pl.ds(at, TOK), :].astype(F32)
                out_ref[pl.ds((i + j) * TOK, TOK), :] = (signal * slope[j * TOK : (j + 1) * TOK]).astype(BF16)

    return pl.pallas_call(
        kernel,
        grid_spec=pltpu.PrefetchScalarGridSpec(
            num_scalar_prefetch=1,
            grid=(COLS // width,),
            in_specs=[pl.BlockSpec((TOK, D), lambda i, p: (0, 0))] * n
            + [pl.BlockSpec((D, width), lambda i, p: (0, i)), pl.BlockSpec((upstream.shape[0], width), lambda i, p: (0, i))],
            out_specs=pl.BlockSpec((n * TOK, width), lambda i, p: (0, i)),
        ),
        out_shape=jax.ShapeDtypeStruct((n * TOK, COLS), BF16),
        compiler_params=pltpu.CompilerParams(vmem_limit_bytes=VMEM),
        cost_estimate=pl.CostEstimate(flops=2 * n * TOK * D * COLS, bytes_accessed=12_000_000, transcendentals=0),
        name="slopes",
    )(first, *blocks, weight, upstream)


def curved(blocks, weight, probe_parts, signals, side, starts, first):
    n, m = len(blocks), len(probe_parts)
    total = sum(b.shape[0] for b in blocks)

    def kernel(side_ref, starts_ref, first_ref, *refs):
        rows_refs, w_ref, probe_refs = refs[:n], refs[n], refs[n + 1 : n + 1 + m]
        mine_ref, other_ref, out_ref, right, signal = refs[n + 1 + m :]
        right[:, :HALF] = w_ref[...]
        for i in range(m):
            at = pl.multiple_of(starts_ref[i], ROWS)
            right[pl.ds(at, probe_parts[i].shape[0]), HALF:] = probe_refs[i][...]
        signal[: 16 * HESS, :] = mine_ref[...]
        signal[16 * HESS :, :] = other_ref[...]
        row = 0
        for i in range(n):
            size = blocks[i].shape[0]
            both = jnp.dot(rows_refs[i][...], right[...], preferred_element_type=F32)
            value = gelu_bend(both[:, :HALF]) * both[:, HALF:]
            for j in range(size // HESS):
                at = pl.multiple_of(first_ref[(row + j * HESS) // HESS], HESS)
                weight_of = signal[pl.ds(at, HESS), :].astype(F32)
                out_ref[pl.ds(row + j * HESS, HESS), :] = (weight_of * value[j * HESS : (j + 1) * HESS]).astype(BF16)
            row += size

    whole = lambda shape: pl.BlockSpec(shape, lambda i, *p: (0, 0))
    return pl.pallas_call(
        kernel,
        grid_spec=pltpu.PrefetchScalarGridSpec(
            num_scalar_prefetch=3,
            grid=(1,),
            in_specs=[whole(b.shape) for b in blocks]
            + [pl.BlockSpec((D, HALF), lambda i, side, *p: (0, side[0]))]
            + [whole(b.shape) for b in probe_parts]
            + [whole(s.shape) for s in signals],
            out_specs=whole((total, HALF)),
            scratch_shapes=[pltpu.VMEM((D, COLS), BF16), pltpu.VMEM((32 * HESS, HALF), BF16)],
        ),
        out_shape=jax.ShapeDtypeStruct((total, HALF), BF16),
        compiler_params=pltpu.CompilerParams(vmem_limit_bytes=VMEM),
        cost_estimate=pl.CostEstimate(flops=2 * total * D * COLS, bytes_accessed=16_000_000, transcendentals=0),
        name="curved",
    )(side, starts, first, *blocks, weight, *probe_parts, *signals)


def products(blocks, values, which, outs):
    n, m, steps = len(blocks), len(values), len(outs)
    total = sum(b.shape[0] for b in blocks)
    width = values[0].shape[1]
    flat = [part for parts in outs for part in parts]
    shapes = [(r.stop - r.start, c.stop - c.start) for r, c in flat]

    def kernel(which_ref, *refs):
        block_refs, value_refs, out_refs = refs[:n], refs[n : n + m], refs[n + m : n + m + len(flat)]
        left, right = refs[n + m + len(flat) :]
        row = 0
        for i in range(n):
            left[pl.ds(row, blocks[i].shape[0]), :] = block_refs[i][...]
            row += blocks[i].shape[0]

        @pl.when(pl.program_id(0) == 0)
        def _():
            row = 0
            for i in range(m):
                right[pl.ds(row, values[i].shape[0]), :] = value_refs[i][...]
                row += values[i].shape[0]

        result = lax.dot_general(left[...], right[...], (((0,), (0,)), ((), ())), preferred_element_type=F32).astype(BF16)
        at = 0
        for g in range(steps):

            @pl.when(pl.program_id(0) == g)
            def _(at=at, g=g):
                for k, (r, c) in enumerate(outs[g]):
                    out_refs[at + k][...] = result[r, c]

            at += len(outs[g])

    return pl.pallas_call(
        kernel,
        grid_spec=pltpu.PrefetchScalarGridSpec(
            num_scalar_prefetch=1,
            grid=(steps,),
            in_specs=[pl.BlockSpec((b.shape[0], PAIR), lambda i, p: (0, p[i])) for b in blocks]
            + [pl.BlockSpec(v.shape, lambda i, p: (0, 0)) for v in values],
            out_specs=[pl.BlockSpec(s, lambda i, p: (0, 0)) for s in shapes],
            scratch_shapes=[pltpu.VMEM((total, PAIR), BF16), pltpu.VMEM((total, width), BF16)],
        ),
        out_shape=[jax.ShapeDtypeStruct(s, BF16) for s in shapes],
        compiler_params=pltpu.CompilerParams(vmem_limit_bytes=VMEM),
        cost_estimate=pl.CostEstimate(flops=2 * steps * total * PAIR * width, bytes_accessed=8_000_000, transcendentals=0),
        name="products",
    )(which, *blocks, *values)


def add_rows(low, high, extra, lower):
    if lower:
        low = (low.astype(F32) + extra.astype(F32)).astype(BF16)
    else:
        high = (high.astype(F32) + extra.astype(F32)).astype(BF16)
    return jnp.concatenate([low, high], 0)


def ring_sum(far_low, far_high, up, down, own):
    from_down = send(far_low, X_UP)
    from_up = send(far_high, X_DOWN)
    up = add_rows(up[:ROWS], up[ROWS:], from_down, True)
    down = add_rows(down[:ROWS], down[ROWS:], from_up, False)
    first = send(up, X_UP)
    second = send(down, X_DOWN)
    return own, first, second


def rows_of(parts, owner):
    picked = [lax.dynamic_slice_in_dim(p, owner * ROWS, ROWS, 0).astype(F32) for p in parts]
    return sum(picked[1:], picked[0])


def shards(tokens, hess_tokens, upstream, hess_upstream, weight, probes, momentum, curvature):
    dp, fsdp = lax.axis_index("dp"), lax.axis_index("fsdp")
    x, y_lo = dp // 2, dp % 2
    y_hi, z, core = fsdp // 8, (fsdp // 2) % 4, fsdp % 2
    y = y_hi * 2 + y_lo

    def columns(value, side):
        return lax.dynamic_slice_in_dim(value, side * HALF, HALF, 1)

    from_y = [send(hess_tokens, s) for s in (Y_UP, Y_DOWN, Y_TWO)]
    hess_y = jnp.concatenate([hess_tokens] + from_y, 0)
    hess_zm = send(hess_y, Z_UP)
    hess_zp = send(hess_y, Z_DOWN)
    hess_za = send(hess_zm[:64], Z_UP)
    hess_zb = send(hess_zp[64:], Z_DOWN)
    hess_own = [hess_y, hess_zm, hess_zp, hess_za, hess_zb]
    hess_blocks = hess_own + [send(b, SWAP) for b in hess_own]

    mine = columns(probes, y_lo)
    other = send(columns(probes, 1 - y_lo), Y_PAIR)
    low = y_lo == 0
    probe_pair = jnp.concatenate([jnp.where(low, mine, other), jnp.where(low, other, mine)], 0)
    probe_m = send(probe_pair, X_UP)
    probe_p = send(probe_pair, X_DOWN)
    probe_a = send(probe_m[:ROWS], X_UP)
    probe_b = send(probe_p[ROWS:], X_DOWN)
    probe_parts = [probe_pair, probe_m, probe_p, probe_a, probe_b]
    signals = [columns(hess_upstream, y_lo), send(columns(hess_upstream, 1 - y_lo), Y_PAIR)]

    tok_m = send(tokens, Z_UP)
    tok_p = send(tokens, Z_DOWN)
    tok_y = send(tokens, Y_TWO)
    tok_2 = jnp.concatenate([send(tok_m[:64], Z_UP), send(tok_p[64:], Z_DOWN)], 0)
    tok_ym = send(tok_y, Z_UP)
    tok_yp = send(tok_y, Z_DOWN)
    tok_y2 = send(tok_2, Y_TWO)
    places = [(0, 0), (0, 3), (0, 1), (1, 0), (0, 2), (1, 3), (1, 1), (1, 2)]
    tok_pairs = [(b, send(b, SWAP)) for b in (tokens, tok_m, tok_p, tok_y, tok_2, tok_ym, tok_yp, tok_y2)]
    token_rows = []
    for step_y, step_z in places:
        at = ((y_hi + step_y) % 2) * 8 + ((z + step_z) % 4) * 2
        token_rows += [(at + core) * TOK, (at + 1 - core) * TOK]
    token_rows = jnp.stack(token_rows).astype(jnp.int32)

    starts = jnp.stack([x * PAIR, ((x + 3) % 4) * PAIR, ((x + 1) % 4) * PAIR, ((x + 2) % 4) * PAIR, ((x + 2) % 4) * PAIR + ROWS])
    hess_rows = []
    for step_core in range(2):
        for step_z, steps_y in ((0, (0, 3, 1, 2)), (3, (0, 3, 1, 2)), (1, (0, 3, 1, 2)), (2, (0, 3)), (2, (1, 2))):
            for step_y in steps_y:
                at_y = (y + step_y) % 4
                place = (at_y // 2) * 8 + ((z + step_z) % 4) * 2 + (core + step_core) % 2
                hess_rows.append(((at_y + y_lo) % 2) * 16 * HESS + place * HESS)
    hess_values = curved(
        hess_blocks,
        weight,
        probe_parts,
        signals,
        y_lo.reshape(1).astype(jnp.int32),
        starts.astype(jnp.int32),
        jnp.stack(hess_rows).astype(jnp.int32),
    )
    all_rows, half_cols = slice(0, PAIR), slice(0, HALF)
    low_rows, high_rows = slice(0, ROWS), slice(ROWS, PAIR)
    targets = jnp.stack([(x + 2) % 4, (x + 1) % 4, (x + 3) % 4, x]).astype(jnp.int32)
    hess_parts = products(
        hess_blocks,
        [hess_values],
        targets,
        [[(low_rows, half_cols), (high_rows, half_cols)]] + [[(all_rows, half_cols)]] * 3,
    )
    hess_sums = ring_sum(*hess_parts)
    hess_other = send(rows_of(hess_sums, 1 - y_lo).astype(BF16), Y_PAIR).astype(F32)
    hess_mine = rows_of(hess_sums, y_lo)
    hessian_vec = jnp.concatenate([jnp.where(low, hess_mine, hess_other), jnp.where(low, hess_other, hess_mine)], 1)
    new_curvature = BETA_TWO * curvature + (1.0 - BETA_TWO) * (probes.astype(F32) * hessian_vec)

    slopes, at = [], 0
    for group in (tok_pairs[:1], tok_pairs[1:4], tok_pairs[4:5], tok_pairs[5:]):
        count = 2 * len(group)
        slopes.append(forward(group, weight, upstream, token_rows[at : at + count]))
        at += count
    tok_blocks = [b for pair in tok_pairs for b in pair]
    sides = (slice(0, HALF), slice(HALF, COLS))
    far = products(tok_blocks, slopes, targets[:1], [[(r, c) for c in sides for r in (low_rows, high_rows)]])
    near = products(tok_blocks, slopes, targets[1:3], [[(all_rows, c) for c in sides]] * 2)
    own = products(tok_blocks, slopes, targets[3:], [[(all_rows, c) for c in sides]])
    gradient = []
    for k in range(2):
        sums = ring_sum(far[2 * k], far[2 * k + 1], near[k], near[2 + k], own[k])
        passed = send(rows_of(sums, 1 - y_lo).astype(BF16), Y_PAIR).astype(F32)
        gradient.append(rows_of(sums, y_lo) + passed)
    gradient = jnp.concatenate(gradient, 1)

    own_weight = lax.dynamic_slice_in_dim(weight, dp * ROWS, ROWS, 0)
    new_momentum = BETA_ONE * momentum + (1.0 - BETA_ONE) * gradient
    ratio = jnp.clip(new_momentum / jnp.maximum(HESS_SCALE * new_curvature, RATIO_FLOOR), -1.0, 1.0)
    new_weight = (own_weight.astype(F32) * (1.0 - LEARN_RATE * WEIGHT_DECAY) - LEARN_RATE * ratio).astype(BF16)
    return (new_weight, new_momentum, new_curvature)


def solution(mesh):
    return jax.shard_map(
        shards,
        mesh=mesh,
        in_specs=(
            P(("dp", "fsdp"), None),
            P(("dp", "fsdp"), None),
            P("dp", "fsdp"),
            P("dp", "fsdp"),
            P(None, "fsdp"),
            P("dp", "fsdp"),
            P("dp", "fsdp"),
            P("dp", "fsdp"),
        ),
        out_specs=(P("dp", "fsdp"), P("dp", "fsdp"), P("dp", "fsdp")),
        check_vma=False,
    )
```

```python
import math

import jax
import jax.numpy as jnp
from jax import lax
from jax.experimental import pallas as pl
from jax.experimental.pallas import tpu as pltpu
from jax.sharding import PartitionSpec as P

SQRT_HALF = 1.0 / math.sqrt(2.0)
INV_ROOT_TAU = 1.0 / math.sqrt(2.0 * math.pi)
BETA_ONE = 0.965
BETA_TWO = 0.99
LEARN_RATE = 0.0006
WEIGHT_DECAY = 0.1
HESS_SCALE = 0.01
RATIO_FLOOR = 0.001

D = 3072
COLS = 768
HALF = COLS // 2
ROWS = 384
PAIR = 2 * ROWS
TOK = 128
HESS = 32
VMEM = 30 << 20
AXES = ("x", "y_lo", "y_hi", "z", "core")
SIZES = (4, 2, 2, 4, 2)
BF16 = jnp.bfloat16
F32 = jnp.float32


def device_index(x, y, z, core):
    return (x * 2 + y % 2) * 16 + (y // 2) * 8 + z * 2 + core


def moves(step):
    pairs = []
    for x in range(4):
        for y in range(4):
            for z in range(4):
                for core in range(2):
                    if step == "y^":
                        to = (x, y ^ 1, z, core)
                    elif step == "x by core":
                        to = ((x + 1 - 2 * core) % 4, y, z, core)
                    elif step == "z by core":
                        to = (x, y, (z + 1 - 2 * core) % 4, core)
                    else:
                        to = ((x + step[0]) % 4, (y + step[1]) % 4, (z + step[2]) % 4, (core + step[3]) % 2)
                    pairs.append((device_index(x, y, z, core), device_index(*to)))
    return pairs


X_UP, X_DOWN, X_TWO = (1, 0, 0, 0), (3, 0, 0, 0), (2, 0, 0, 0)
Y_UP, Y_DOWN, Y_TWO = (0, 1, 0, 0), (0, 3, 0, 0), (0, 2, 0, 0)
Z_UP, Z_DOWN = (0, 0, 1, 0), (0, 0, 3, 0)
SWAP = (0, 0, 0, 1)
Y_PAIR = "y^"
X_CORE, Z_CORE = "x by core", "z by core"


def send(value, step):
    return lax.ppermute(value, AXES, moves(step))


def gelu_slope(preact):
    normal_cdf = 0.5 * (1.0 + lax.erf(preact * SQRT_HALF))
    density = jnp.exp(-0.5 * preact * preact) * INV_ROOT_TAU
    return normal_cdf + preact * density


def gelu_bend(preact):
    density = jnp.exp(-0.5 * preact * preact) * INV_ROOT_TAU
    return density * (2.0 - preact * preact)


def cost(microseconds):
    return pl.CostEstimate(flops=int(microseconds * 1_000_000_000), bytes_accessed=1000, transcendentals=0)


def after(value, *others):
    return lax.optimization_barrier((value, *others))[0]


ANY = pl.BlockSpec(memory_space=pl.ANY)


class Copies:
    def __init__(self, sems, first=0):
        self.sems, self.next, self.held = sems, first, []

    def start(self, source, target):
        copy = pltpu.make_async_copy(source, target, self.sems.at[self.next])
        copy.start()
        self.next += 1
        self.held.append(copy)

    def wait(self):
        for copy in self.held:
            copy.wait()
        self.held = []


def forward(blocks, weight, upstream, scalars, first):
    first = scalars[1][first]
    n, width, piece = len(blocks), 256, D // 4
    total = sum(rows for _, _, rows in blocks)
    count = total // TOK

    def kernel(first_ref, *refs):
        tokens, w_ref, u_ref, out_ref = refs[:n], refs[n], refs[n + 1], refs[n + 2]
        rows_all, right, signal, sems = refs[n + 3 :]
        some = Copies(sems)

        def fetch(block):
            for k in range(4):
                rows = pl.ds(k * piece, piece)
                some.start(w_ref.at[rows, pl.ds(block * width, width)], right.at[block, rows, :])

        at = 0
        fetch(0)
        for ref, (_, row, rows) in zip(tokens, blocks):
            for j in range(0, rows, TOK):
                some.start(ref.at[pl.ds(row + j, TOK), :], rows_all.at[pl.ds(at + j, TOK), :])
            at += rows
        for j in range(count):
            begin = pl.multiple_of(first_ref[first + j], TOK)
            some.start(u_ref.at[pl.ds(begin, TOK), :], signal.at[pl.ds(j * TOK, TOK), :])
        some.wait()
        for block in range(COLS // width):
            if block + 1 < COLS // width:
                fetch(block + 1)
            cols = slice(block * width, (block + 1) * width)
            for row in range(0, total, 256):
                size = min(256, total - row)
                pre = jnp.dot(rows_all[row : row + size, :], right[block], preferred_element_type=F32)
                value = signal[row : row + size, cols].astype(F32) * gelu_slope(pre)
                out_ref[cols, row : row + size] = value.T.astype(BF16)
            some.wait()

    return pl.pallas_call(
        kernel,
        grid_spec=pltpu.PrefetchScalarGridSpec(
            num_scalar_prefetch=1,
            grid=(1,),
            in_specs=[ANY] * (n + 2),
            out_specs=pl.BlockSpec((COLS, total), lambda i, p: (0, 0)),
            scratch_shapes=[
                pltpu.VMEM((total, D), BF16),
                pltpu.VMEM((COLS // width, D, width), BF16),
                pltpu.VMEM((total, COLS), BF16),
                pltpu.SemaphoreType.DMA((12 + 2 * count,)),
            ],
        ),
        out_shape=jax.ShapeDtypeStruct((COLS, total), BF16),
        compiler_params=pltpu.CompilerParams(vmem_limit_bytes=VMEM),
        cost_estimate=cost(2 + total / 160),
        name="slopes",
    )(scalars[0], *[b for b, _, _ in blocks], weight, upstream)


def curved(blocks, weight, probe_parts, signals, scalars, first):
    n, m = len(blocks), len(probe_parts)
    total = sum(rows for _, _, rows in blocks)
    held = 16 * HESS
    side, starts, first = (scalars[1][name] for name in ("side", "starts", first))

    def kernel(ref_of, *refs):
        rows_refs, w_ref, probe_refs = refs[:n], refs[n], refs[n + 1 : n + 1 + m]
        mine_ref, other_ref, out_ref, right, rows_all, signal, sems = refs[n + 1 + m :]
        some = Copies(sems)
        half = pl.ds(pl.multiple_of(ref_of[side] * HALF, HALF), HALF)
        for k in range(4):
            rows = pl.ds(k * PAIR, PAIR)
            some.start(w_ref.at[rows, half], right.at[rows, pl.ds(0, HALF)])
        for i in range(m):
            rows = pl.ds(pl.multiple_of(ref_of[starts + i], PAIR), PAIR)
            some.start(probe_refs[i], right.at[rows, pl.ds(HALF, HALF)])
        at = 0
        for ref, (_, row, rows) in zip(rows_refs, blocks):
            for j in range(0, rows, 128):
                some.start(ref.at[pl.ds(row + j, 128), :], rows_all.at[pl.ds(at + j, 128), :])
            at += rows
        some.start(mine_ref.at[:, half], signal.at[pl.ds(0, held), :])
        some.start(other_ref.at[pl.ds(ROWS, held), :], signal.at[pl.ds(held, held), :])
        some.wait()
        for row in range(0, total, 256):
            both = jnp.dot(rows_all[row : row + 256, :], right[...], preferred_element_type=F32)
            value = gelu_bend(both[:, :HALF]) * both[:, HALF:]
            signs = []
            for j in range(256 // HESS):
                at = pl.multiple_of(ref_of[first + row // HESS + j], HESS)
                signs.append(signal[pl.ds(at, HESS), :].astype(F32))
            out_ref[:, row : row + 256] = (jnp.concatenate(signs, 0) * value).T.astype(BF16)

    return pl.pallas_call(
        kernel,
        grid_spec=pltpu.PrefetchScalarGridSpec(
            num_scalar_prefetch=1,
            grid=(1,),
            in_specs=[ANY] * (n + 3 + m),
            out_specs=pl.BlockSpec((HALF, total), lambda i, *p: (0, 0)),
            scratch_shapes=[
                pltpu.VMEM((D, COLS), BF16),
                pltpu.VMEM((total, D), BF16),
                pltpu.VMEM((2 * held, HALF), BF16),
                pltpu.SemaphoreType.DMA((6 + m + total // 128,)),
            ],
        ),
        out_shape=jax.ShapeDtypeStruct((HALF, total), BF16),
        compiler_params=pltpu.CompilerParams(vmem_limit_bytes=VMEM),
        cost_estimate=cost(3 + total / 128),
        name="curved",
    )(scalars[0], *[b for b, _, _ in blocks], weight, *probe_parts, *signals)


def products(blocks, values, scalars, which, shapes, outs):
    n, m, steps, count = len(blocks), len(values), len(outs), len(shapes)
    total = sum(rows for _, _, rows in blocks)
    height = values[0].shape[0]
    which, side = scalars[1]["targets"] + which, scalars[1]["side"]

    def kernel(ref_of, *refs):
        block_refs, value_refs, out_refs = refs[:n], refs[n : n + m], refs[n + m :]
        left = jnp.concatenate([r[...] for r in value_refs], 1)
        right = jnp.concatenate([r[...] for r in block_refs], 0)
        result = jnp.dot(left, right, preferred_element_type=F32).astype(BF16)
        for k in range(steps):

            @pl.when(pl.program_id(0) == k)
            def _(k=k):
                for out, begin, r, c in outs[k]:
                    if isinstance(c, str):
                        low = (ref_of[side] == 0) == (c == "own")
                        value = jnp.where(low, result[r, :ROWS], result[r, ROWS:])
                    else:
                        value = result[r, c]
                    out_refs[out][begin : begin + r.stop - r.start, :] = value

    return pl.pallas_call(
        kernel,
        grid_spec=pltpu.PrefetchScalarGridSpec(
            num_scalar_prefetch=1,
            grid=(steps,),
            in_specs=[pl.BlockSpec((rows, PAIR), lambda i, p, b=row // rows: (b, p[which + i])) for _, row, rows in blocks]
            + [pl.BlockSpec(v.shape, lambda i, p: (0, 0)) for v in values],
            out_specs=[pl.BlockSpec(s, lambda i, p: (0, 0)) for s in shapes],
        ),
        out_shape=[jax.ShapeDtypeStruct(s, BF16) for s in shapes],
        compiler_params=pltpu.CompilerParams(vmem_limit_bytes=VMEM),
        cost_estimate=cost(2 + 2.5 * steps * height * total / (768 * 2048)),
        name="products",
    )(scalars[0], *[b for b, _, _ in blocks], *values)


def plus(left, right):
    return (left.astype(F32) + right.astype(F32)).astype(BF16)


def share(part, scalars, step):
    side = scalars[1]["side"]
    if part.shape[1] == PAIR:
        return pl.BlockSpec((part.shape[0], step), lambda i, s: (0, s[side] * (ROWS // step) + i))
    return pl.BlockSpec((part.shape[0], step), lambda i, s: (0, i))


def curvature_update(scalars, bends, curvature, probes):
    step, side = 128, scalars[1]["side"]

    def kernel(ref_of, *refs):
        c_ref, p_ref, new_c = refs[len(bends) :]
        values = [ref[...].astype(F32) for ref in refs[: len(bends)]]
        mine, other = sum(values[1:-1], values[0]), values[-1]
        low = ref_of[side] == 0
        bend = jnp.concatenate([jnp.where(low, mine, other), jnp.where(low, other, mine)], 0).T
        new_c[...] = BETA_TWO * c_ref[...] + (1.0 - BETA_TWO) * (p_ref[...].astype(F32) * bend)

    state = pl.BlockSpec((step, COLS), lambda i, s: (i, 0))
    return pl.pallas_call(
        kernel,
        grid_spec=pltpu.PrefetchScalarGridSpec(
            num_scalar_prefetch=1,
            grid=(ROWS // step,),
            in_specs=[share(p, scalars, step) for p in bends] + [state] * 2,
            out_specs=state,
        ),
        out_shape=jax.ShapeDtypeStruct((ROWS, COLS), F32),
        compiler_params=pltpu.CompilerParams(vmem_limit_bytes=VMEM),
        cost_estimate=cost(4),
        name="curvature",
    )(scalars[0], *bends, curvature, probes)


def update(scalars, late, early, momentum, curvature, weight):
    parts = late + early
    split, step, dp = len(late), 128, scalars[1]["dp"]

    def kernel(ref_of, *refs):
        values = [ref[...].astype(F32) for ref in refs[: len(parts)]]
        m_ref, c_ref, w_ref, new_w, new_m = refs[len(parts) :]
        late_sum = sum(values[1:split], values[0])
        early_sum = sum(values[split + 1 :], values[split])
        gradient = jnp.concatenate([early_sum, late_sum], 0).T
        mom = BETA_ONE * m_ref[...] + (1.0 - BETA_ONE) * gradient
        ratio = jnp.clip(mom / jnp.maximum(HESS_SCALE * c_ref[...], RATIO_FLOOR), -1.0, 1.0)
        new_w[...] = (w_ref[...].astype(F32) * (1.0 - LEARN_RATE * WEIGHT_DECAY) - LEARN_RATE * ratio).astype(BF16)
        new_m[...] = mom

    state = pl.BlockSpec((step, COLS), lambda i, s: (i, 0))
    return pl.pallas_call(
        kernel,
        grid_spec=pltpu.PrefetchScalarGridSpec(
            num_scalar_prefetch=1,
            grid=(ROWS // step,),
            in_specs=[share(p, scalars, step) for p in parts]
            + [state] * 2
            + [pl.BlockSpec((step, COLS), lambda i, s: (s[dp] * (ROWS // step) + i, 0))],
            out_specs=[state] * 2,
        ),
        out_shape=[jax.ShapeDtypeStruct((ROWS, COLS), t) for t in (BF16, F32)],
        compiler_params=pltpu.CompilerParams(vmem_limit_bytes=VMEM),
        cost_estimate=cost(4),
        name="update",
    )(scalars[0], *parts, momentum, curvature, weight)


def shards(tokens, hess_tokens, upstream, hess_upstream, weight, probes, momentum, curvature):
    x, y_lo, y_hi, z, core = (lax.axis_index(a) for a in AXES)
    low = y_lo == 0

    def columns(value, own):
        first, last = value[:, :HALF], value[:, HALF:]
        return jnp.where(low, first, last) if own else jnp.where(low, last, first)

    def token_rows(places):
        rows = []
        for step_core, step_y, step_z in places:
            at = ((y_hi + step_y) % 2) * 8 + ((z + step_z) % 4) * 2 + (core + step_core) % 2
            rows.append(TOK * at)
        return rows

    def hess_rows(*groups):
        rows = []
        for steps_z, step_core in [(steps_z, c) for steps_z in groups for c in (0, 1)]:
            for step_z, step_y in [(a, b) for a in steps_z for b in (0, 3, 1, 2)]:
                at_y = (y_hi * 2 + y_lo + step_y) % 4
                place = (at_y // 2) * 8 + ((z + step_z) % 4) * 2 + (core + step_core) % 2
                rows.append(((at_y + y_lo) % 2) * 16 * HESS + place * HESS)
        return rows

    up_first = [3 + 2 * ((core + c) % 2) for c in (0, 1)]
    down_first = [1 + 2 * ((core + c) % 2) for c in (0, 1)]
    groups = {
        "side": [y_lo],
        "dp": [x * 2 + y_lo],
        "targets": [(x + 2) % 4, (x + 1) % 4, (x + 3) % 4, x],
        "starts": [x * PAIR, (x + 3) % 4 * PAIR, (x + 1) % 4 * PAIR, (x + 2) % 4 * PAIR],
        "one": token_rows([(c, 0, b) for c in (0, 1) for b in (up_first[c], 0, down_first[c])]),
        "two": token_rows(
            [(c, 1, b) for c in (0, 1) for b in (up_first[c], 0)]
        ),
        "three": token_rows(
            [(c, 0, 2) for c in (0, 1)] + [(c, 1, down_first[c]) for c in (0, 1)] + [(c, 1, 2) for c in (0, 1)]
        ),
        "hess": hess_rows((0, 3, 1), (2,)),
    }
    places, at = {}, 0
    for name, group in groups.items():
        places[name] = at
        at += len(group)
    scalars = (jnp.stack([v for group in groups.values() for v in group]).astype(jnp.int32), places)

    hess_ym = send(hess_tokens, Y_UP)
    hess_yp = send(hess_tokens, Y_DOWN)
    hess_y2 = send(hess_tokens, Y_TWO)
    tok_m = send(tokens, Z_UP)
    tok_p = send(tokens, Z_DOWN)
    hess_y = jnp.concatenate([hess_tokens, hess_ym, hess_yp, hess_y2], 0)
    two_b = send(after(tokens, hess_y), Y_TWO)
    hess_y, tok_m, tok_p, two_b = lax.optimization_barrier((hess_y, tok_m, tok_p, two_b))

    hess_m = send(hess_y, Z_UP)
    hess_p = send(hess_y, Z_DOWN)
    pair = send(jnp.concatenate([columns(probes, False), columns(hess_upstream, False)], 0), Y_PAIR)
    tok_a, tok_b = jnp.where(core == 0, tok_m, tok_p), jnp.where(core == 0, tok_p, tok_m)
    tok_one = jnp.concatenate([tok_a, after(tokens, hess_y), tok_b], 0)
    tok_one_swap = send(tok_one, SWAP)
    slopes_one = forward([(tok_one, 0, 384), (tok_one_swap, 0, 384)], weight, upstream, scalars, "one")
    hess_m, hess_p, pair, slopes_one = lax.optimization_barrier((hess_m, hess_p, pair, slopes_one))

    far = jnp.concatenate([jnp.where(core == 0, hess_m, hess_p), tok_a], 0)
    mine, other = columns(probes, True), pair[:ROWS]
    probe_pair = jnp.concatenate([jnp.where(low, mine, other), jnp.where(low, other, mine)], 0)
    hess_near = jnp.concatenate([after(hess_y, far, probe_pair), hess_m, hess_p], 0)
    far = send(far, Z_CORE)
    two_a = send(after(tok_a, pair), Y_TWO)
    probe_m = send(probe_pair, X_UP)
    probe_p = send(probe_pair, X_DOWN)
    near_swap = send(hess_near, SWAP)
    far, two_a, probe_m, probe_p, near_swap = lax.optimization_barrier((far, two_a, probe_m, probe_p, near_swap))

    last = send(two_a, Z_CORE)
    three = send(after(tok_b, two_a), Y_TWO)
    probe_2 = send(jnp.where(core == 0, probe_m, probe_p), X_CORE)
    far_swap = send(far, SWAP)
    two = jnp.concatenate([two_a, two_b], 0)
    two_toks = [(r, 0, 256) for r in (two, send(two, SWAP))]
    slopes_two = forward(two_toks, weight, upstream, scalars, "two")
    probe_parts = [probe_pair, probe_m, probe_p, probe_2]
    hess_blocks = [(hess_near, 0, 384), (near_swap, 0, 384), (far, 0, 128), (far_swap, 0, 128)]
    hess_values = curved(hess_blocks, weight, probe_parts, [hess_upstream, pair], scalars, "hess")
    half, whole = slice(0, HALF), slice(0, PAIR)
    hess_2, hess_up, hess_down, hess_own = products(
        hess_blocks,
        [hess_values],
        scalars,
        0,
        [(HALF, PAIR)] * 4,
        [[(g, 0, half, whole)] for g in range(4)],
    )
    three, last, slopes_two, hess_2, hess_up, hess_down = lax.optimization_barrier(
        (three, last, slopes_two, hess_2, hess_up, hess_down)
    )
    three_swap = send(three, SWAP)
    last_swap = send(last, SWAP)
    hess_2 = send(hess_2, X_CORE)
    three_toks = [(r, r.shape[0] - 128, 128) for r in (far, far_swap, three, three_swap, last, last_swap)]
    slopes_three = forward(three_toks, weight, upstream, scalars, "three")
    hess_2, slopes_three = lax.optimization_barrier((hess_2, slopes_three))
    hess_up = plus(hess_up, jnp.where(core == 0, hess_2, 0))
    hess_down = plus(hess_down, jnp.where(core == 0, 0, hess_2))
    slopes_three = after(slopes_three, hess_up, hess_down)
    bends = [hess_own, send(hess_up, X_UP), send(hess_down, X_DOWN)]

    def for_other(parts):
        picked = [jnp.where(low, p[:, ROWS:], p[:, :ROWS]).astype(F32) for p in parts]
        return send(sum(picked[1:], picked[0]).astype(BF16), Y_PAIR)

    tok_blocks = [(tok_one, 0, 384), (tok_one_swap, 0, 384)] + two_toks + three_toks
    slopes = [slopes_one, slopes_two, slopes_three]
    first, rest = slice(0, 256), slice(256, COLS)
    far_share, far_other, far_own = products(
        tok_blocks,
        slopes,
        scalars,
        0,
        [(512, PAIR)] + [(256, ROWS)] * 2,
        [[(0, 0, rest, whole), (1, 0, first, "other"), (2, 0, first, "own")]],
    )
    order, far_other, *bends[1:] = lax.optimization_barrier((scalars[0], far_other, *bends[1:]))
    far_share = send(far_share, X_CORE)
    far_pair = send(far_other, Y_PAIR)
    up, down, own, near_other, near_own = products(
        tok_blocks,
        slopes,
        (order, places),
        1,
        [(512, PAIR)] * 3 + [(768, ROWS)] * 2,
        [[(g, 0, rest, whole), (3, g * 256, first, "other"), (4, g * 256, first, "own")] for g in range(3)],
    )
    near_pair = send(near_other, Y_PAIR)
    far_share, far_pair, up, down = lax.optimization_barrier((far_share, far_pair, up, down))
    up = plus(up, jnp.where(core == 0, far_share, 0))
    down = plus(down, jnp.where(core == 0, 0, far_share))
    late = [own, send(up, X_UP), send(down, X_DOWN)]
    early = [
        send(plus(far_own, far_pair), X_TWO),
        send(plus(near_own[:256], near_pair[:256]), X_UP),
        send(plus(near_own[256:512], near_pair[256:512]), X_DOWN),
        near_own[512:],
        near_pair[512:],
    ]
    bends.append(for_other(bends))
    new_curvature = curvature_update(scalars, bends, curvature, probes)
    late[1], late[2], early[0], new_curvature = lax.optimization_barrier((late[1], late[2], early[0], new_curvature))
    late.append(for_other(late))
    new_weight, new_momentum = update(scalars, late, early, momentum, new_curvature, weight)
    return new_weight, new_momentum, new_curvature


def solution(mesh):
    split = jax.sharding.Mesh(mesh.devices.reshape(SIZES), AXES)
    dp, fsdp = AXES[:2], AXES[2:]
    state = P(dp, fsdp)
    return jax.shard_map(
        shards,
        mesh=split,
        in_specs=(P(AXES, None), P(AXES, None), state, state, P(None, fsdp), state, state, state),
        out_specs=(state, state, state),
        check_vma=False,
    )
```

```python
import math

import jax
import jax.numpy as jnp
from jax import lax
from jax.experimental import pallas as pl
from jax.experimental.pallas import tpu as pltpu
from jax.sharding import PartitionSpec as P

SQRT_HALF = 1.0 / math.sqrt(2.0)
INV_ROOT_TAU = 1.0 / math.sqrt(2.0 * math.pi)
BETA_ONE = 0.965
BETA_TWO = 0.99
LEARN_RATE = 0.0006
WEIGHT_DECAY = 0.1
HESS_SCALE = 0.01
RATIO_FLOOR = 0.001

D = 3072
COLS = 768
HALF = COLS // 2
ROWS = 384
PAIR = 2 * ROWS
TOK = 128
HESS = 32
VMEM = 30 << 20
AXES = ("x", "y_lo", "y_hi", "z", "core")
SIZES = (4, 2, 2, 4, 2)
BF16 = jnp.bfloat16
F32 = jnp.float32


def device_index(x, y, z, core):
    return (x * 2 + y % 2) * 16 + (y // 2) * 8 + z * 2 + core


def moves(step):
    pairs = []
    for x in range(4):
        for y in range(4):
            for z in range(4):
                for core in range(2):
                    if step == "y^":
                        to = (x, y ^ 1, z, core)
                    elif step == "x by core":
                        to = ((x + 1 - 2 * core) % 4, y, z, core)
                    elif step == "z by core":
                        to = (x, y, (z + 1 - 2 * core) % 4, core)
                    else:
                        to = ((x + step[0]) % 4, (y + step[1]) % 4, (z + step[2]) % 4, (core + step[3]) % 2)
                    pairs.append((device_index(x, y, z, core), device_index(*to)))
    return pairs


X_UP, X_DOWN, X_TWO = (1, 0, 0, 0), (3, 0, 0, 0), (2, 0, 0, 0)
Y_UP, Y_DOWN, Y_TWO = (0, 1, 0, 0), (0, 3, 0, 0), (0, 2, 0, 0)
Z_UP, Z_DOWN = (0, 0, 1, 0), (0, 0, 3, 0)
SWAP = (0, 0, 0, 1)
Y_PAIR = "y^"
X_CORE, Z_CORE = "x by core", "z by core"


def send(value, step):
    return lax.ppermute(value, AXES, moves(step))


def gelu_slope(preact):
    normal_cdf = 0.5 * (1.0 + lax.erf(preact * SQRT_HALF))
    density = jnp.exp(-0.5 * preact * preact) * INV_ROOT_TAU
    return normal_cdf + preact * density


def gelu_bend(preact):
    density = jnp.exp(-0.5 * preact * preact) * INV_ROOT_TAU
    return density * (2.0 - preact * preact)


def cost(microseconds):
    return pl.CostEstimate(flops=int(microseconds * 1_000_000_000), bytes_accessed=1000, transcendentals=0)


def after(value, *others):
    return lax.optimization_barrier((value, *others))[0]


ANY = pl.BlockSpec(memory_space=pl.ANY)


class Copies:
    def __init__(self, sems, first=0):
        self.sems, self.next, self.held = sems, first, []

    def start(self, source, target):
        copy = pltpu.make_async_copy(source, target, self.sems.at[self.next])
        copy.start()
        self.next += 1
        self.held.append(copy)

    def wait(self):
        for copy in self.held:
            copy.wait()
        self.held = []


def forward(blocks, weight, upstream, scalars, first):
    first = scalars[1][first]
    n, width, piece = len(blocks), 256, D // 4
    total = sum(rows for _, _, rows in blocks)
    count = total // TOK

    def kernel(first_ref, *refs):
        tokens, w_ref, u_ref, out_ref = refs[:n], refs[n], refs[n + 1], refs[n + 2]
        rows_all, right, signal, sems = refs[n + 3 :]
        some = Copies(sems)

        def fetch(block):
            for k in range(4):
                rows = pl.ds(k * piece, piece)
                some.start(w_ref.at[rows, pl.ds(block * width, width)], right.at[block, rows, :])

        at = 0
        fetch(0)
        for ref, (_, row, rows) in zip(tokens, blocks):
            for j in range(0, rows, TOK):
                some.start(ref.at[pl.ds(row + j, TOK), :], rows_all.at[pl.ds(at + j, TOK), :])
            at += rows
        for j in range(count):
            begin = pl.multiple_of(first_ref[first + j], TOK)
            some.start(u_ref.at[pl.ds(begin, TOK), :], signal.at[pl.ds(j * TOK, TOK), :])
        some.wait()
        for block in range(COLS // width):
            if block + 1 < COLS // width:
                fetch(block + 1)
            cols = slice(block * width, (block + 1) * width)
            for row in range(0, total, 256):
                size = min(256, total - row)
                pre = jnp.dot(rows_all[row : row + size, :], right[block], preferred_element_type=F32)
                value = signal[row : row + size, cols].astype(F32) * gelu_slope(pre)
                out_ref[cols, row : row + size] = value.T.astype(BF16)
            some.wait()

    return pl.pallas_call(
        kernel,
        grid_spec=pltpu.PrefetchScalarGridSpec(
            num_scalar_prefetch=1,
            grid=(1,),
            in_specs=[ANY] * (n + 2),
            out_specs=pl.BlockSpec((COLS, total), lambda i, p: (0, 0)),
            scratch_shapes=[
                pltpu.VMEM((total, D), BF16),
                pltpu.VMEM((COLS // width, D, width), BF16),
                pltpu.VMEM((total, COLS), BF16),
                pltpu.SemaphoreType.DMA((12 + 2 * count,)),
            ],
        ),
        out_shape=jax.ShapeDtypeStruct((COLS, total), BF16),
        compiler_params=pltpu.CompilerParams(vmem_limit_bytes=VMEM),
        cost_estimate=cost(2 + total / 160),
        name="slopes",
    )(scalars[0], *[b for b, _, _ in blocks], weight, upstream)


def curved(blocks, weight, probe_parts, signals, scalars, first):
    n, m = len(blocks), len(probe_parts)
    total = sum(rows for _, _, rows in blocks)
    held = 16 * HESS
    side, starts, first = (scalars[1][name] for name in ("side", "starts", first))

    def kernel(ref_of, *refs):
        rows_refs, w_ref, probe_refs = refs[:n], refs[n], refs[n + 1 : n + 1 + m]
        mine_ref, other_ref, out_ref, right, rows_all, signal, sems = refs[n + 1 + m :]
        some = Copies(sems)
        half = pl.ds(pl.multiple_of(ref_of[side] * HALF, HALF), HALF)
        for k in range(4):
            rows = pl.ds(k * PAIR, PAIR)
            some.start(w_ref.at[rows, half], right.at[rows, pl.ds(0, HALF)])
        for i in range(m):
            rows = pl.ds(pl.multiple_of(ref_of[starts + i], PAIR), PAIR)
            some.start(probe_refs[i], right.at[rows, pl.ds(HALF, HALF)])
        at = 0
        for ref, (_, row, rows) in zip(rows_refs, blocks):
            for j in range(0, rows, 128):
                some.start(ref.at[pl.ds(row + j, 128), :], rows_all.at[pl.ds(at + j, 128), :])
            at += rows
        some.start(mine_ref.at[:, half], signal.at[pl.ds(0, held), :])
        some.start(other_ref.at[pl.ds(ROWS, held), :], signal.at[pl.ds(held, held), :])
        some.wait()
        for row in range(0, total, 256):
            both = jnp.dot(rows_all[row : row + 256, :], right[...], preferred_element_type=F32)
            value = gelu_bend(both[:, :HALF]) * both[:, HALF:]
            signs = []
            for j in range(256 // HESS):
                at = pl.multiple_of(ref_of[first + row // HESS + j], HESS)
                signs.append(signal[pl.ds(at, HESS), :].astype(F32))
            out_ref[:, row : row + 256] = (jnp.concatenate(signs, 0) * value).T.astype(BF16)

    return pl.pallas_call(
        kernel,
        grid_spec=pltpu.PrefetchScalarGridSpec(
            num_scalar_prefetch=1,
            grid=(1,),
            in_specs=[ANY] * (n + 3 + m),
            out_specs=pl.BlockSpec((HALF, total), lambda i, *p: (0, 0)),
            scratch_shapes=[
                pltpu.VMEM((D, COLS), BF16),
                pltpu.VMEM((total, D), BF16),
                pltpu.VMEM((2 * held, HALF), BF16),
                pltpu.SemaphoreType.DMA((6 + m + total // 128,)),
            ],
        ),
        out_shape=jax.ShapeDtypeStruct((HALF, total), BF16),
        compiler_params=pltpu.CompilerParams(vmem_limit_bytes=VMEM),
        cost_estimate=cost(0.1),
        name="curved",
    )(scalars[0], *[b for b, _, _ in blocks], weight, *probe_parts, *signals)


def products(blocks, values, scalars, which, shapes, outs):
    n, m, steps, count = len(blocks), len(values), len(outs), len(shapes)
    total = sum(rows for _, _, rows in blocks)
    height = values[0].shape[0]
    which, side = scalars[1]["targets"] + which, scalars[1]["side"]

    def kernel(ref_of, *refs):
        block_refs, value_refs, out_refs = refs[:n], refs[n : n + m], refs[n + m :]
        left = jnp.concatenate([r[...] for r in value_refs], 1)
        right = jnp.concatenate([r[...] for r in block_refs], 0)
        result = jnp.dot(left, right, preferred_element_type=F32).astype(BF16)
        for k in range(steps):

            @pl.when(pl.program_id(0) == k)
            def _(k=k):
                for out, begin, r, c in outs[k]:
                    if isinstance(c, str):
                        low = (ref_of[side] == 0) == (c == "own")
                        value = jnp.where(low, result[r, :ROWS], result[r, ROWS:])
                    else:
                        value = result[r, c]
                    out_refs[out][begin : begin + r.stop - r.start, :] = value

    return pl.pallas_call(
        kernel,
        grid_spec=pltpu.PrefetchScalarGridSpec(
            num_scalar_prefetch=1,
            grid=(steps,),
            in_specs=[pl.BlockSpec((rows, PAIR), lambda i, p, b=row // rows: (b, p[which + i])) for _, row, rows in blocks]
            + [pl.BlockSpec(v.shape, lambda i, p: (0, 0)) for v in values],
            out_specs=[pl.BlockSpec(s, lambda i, p: (0, 0)) for s in shapes],
        ),
        out_shape=[jax.ShapeDtypeStruct(s, BF16) for s in shapes],
        compiler_params=pltpu.CompilerParams(vmem_limit_bytes=VMEM),
        cost_estimate=cost(0.1 if height == HALF or steps > 1 else 2 + 2.5 * steps),
        name="products",
    )(scalars[0], *[b for b, _, _ in blocks], *values)


def plus(left, right):
    return (left.astype(F32) + right.astype(F32)).astype(BF16)


def share(part, scalars, step):
    side = scalars[1]["side"]
    if part.shape[1] == PAIR:
        return pl.BlockSpec((part.shape[0], step), lambda i, s: (0, s[side] * (ROWS // step) + i))
    return pl.BlockSpec((part.shape[0], step), lambda i, s: (0, i))


def curvature_update(scalars, bends, curvature, probes):
    step, side = 128, scalars[1]["side"]

    def kernel(ref_of, *refs):
        c_ref, p_ref, new_c = refs[len(bends) :]
        values = [ref[...].astype(F32) for ref in refs[: len(bends)]]
        mine, other = sum(values[1:-1], values[0]), values[-1]
        low = ref_of[side] == 0
        bend = jnp.concatenate([jnp.where(low, mine, other), jnp.where(low, other, mine)], 0).T
        new_c[...] = BETA_TWO * c_ref[...] + (1.0 - BETA_TWO) * (p_ref[...].astype(F32) * bend)

    state = pl.BlockSpec((step, COLS), lambda i, s: (i, 0))
    return pl.pallas_call(
        kernel,
        grid_spec=pltpu.PrefetchScalarGridSpec(
            num_scalar_prefetch=1,
            grid=(ROWS // step,),
            in_specs=[share(p, scalars, step) for p in bends] + [state] * 2,
            out_specs=state,
        ),
        out_shape=jax.ShapeDtypeStruct((ROWS, COLS), F32),
        compiler_params=pltpu.CompilerParams(vmem_limit_bytes=VMEM),
        cost_estimate=cost(4),
        name="curvature",
    )(scalars[0], *bends, curvature, probes)


def update(scalars, late, early, momentum, curvature, weight):
    parts = late + early
    split, step, dp = len(late), 128, scalars[1]["dp"]

    def kernel(ref_of, *refs):
        values = [ref[...].astype(F32) for ref in refs[: len(parts)]]
        m_ref, c_ref, w_ref, new_w, new_m = refs[len(parts) :]
        late_sum = sum(values[1:split], values[0])
        early_sum = sum(values[split + 1 :], values[split])
        gradient = jnp.concatenate([early_sum, late_sum], 0).T
        mom = BETA_ONE * m_ref[...] + (1.0 - BETA_ONE) * gradient
        ratio = jnp.clip(mom / jnp.maximum(HESS_SCALE * c_ref[...], RATIO_FLOOR), -1.0, 1.0)
        new_w[...] = (w_ref[...].astype(F32) * (1.0 - LEARN_RATE * WEIGHT_DECAY) - LEARN_RATE * ratio).astype(BF16)
        new_m[...] = mom

    state = pl.BlockSpec((step, COLS), lambda i, s: (i, 0))
    return pl.pallas_call(
        kernel,
        grid_spec=pltpu.PrefetchScalarGridSpec(
            num_scalar_prefetch=1,
            grid=(ROWS // step,),
            in_specs=[share(p, scalars, step) for p in parts]
            + [state] * 2
            + [pl.BlockSpec((step, COLS), lambda i, s: (s[dp] * (ROWS // step) + i, 0))],
            out_specs=[state] * 2,
        ),
        out_shape=[jax.ShapeDtypeStruct((ROWS, COLS), t) for t in (BF16, F32)],
        compiler_params=pltpu.CompilerParams(vmem_limit_bytes=VMEM),
        cost_estimate=cost(4),
        name="update",
    )(scalars[0], *parts, momentum, curvature, weight)


def shards(tokens, hess_tokens, upstream, hess_upstream, weight, probes, momentum, curvature):
    x, y_lo, y_hi, z, core = (lax.axis_index(a) for a in AXES)
    low = y_lo == 0

    def columns(value, own):
        first, last = value[:, :HALF], value[:, HALF:]
        return jnp.where(low, first, last) if own else jnp.where(low, last, first)

    def token_rows(places):
        rows = []
        for step_core, step_y, step_z in places:
            at = ((y_hi + step_y) % 2) * 8 + ((z + step_z) % 4) * 2 + (core + step_core) % 2
            rows.append(TOK * at)
        return rows

    def hess_rows(*groups):
        rows = []
        for group, step_core in [(g, c) for g in groups for c in (0, 1)]:
            for other, step_y, step_z in group:
                place = ((y_hi + step_y) % 2) * 8 + ((z + step_z) % 4) * 2 + (core + step_core) % 2
                rows.append(other * 16 * HESS + place * HESS)
        return rows

    groups = {
        "side": [y_lo],
        "dp": [x * 2 + y_lo],
        "targets": [(x + 2) % 4, (x + 1) % 4, (x + 3) % 4, x],
        "starts": [x * PAIR, (x + 3) % 4 * PAIR, (x + 1) % 4 * PAIR, (x + 2) % 4 * PAIR],
        "one": token_rows([(c, a, b) for c in (0, 1) for a, b in ((0, 0), (0, 3), (0, 1), (1, 0))]),
        "two": token_rows([(c, a, b) for c in (0, 1) for a, b in ((0, 2), (1, 3), (1, 1))]),
        "three": token_rows([(c, 1, 2) for c in (0, 1)]),
        "hess near": hess_rows([(o, a, b) for o in (0, 1) for a, b in ((0, 0), (0, 3), (0, 1), (1, 0))]),
        "hess rest": hess_rows([(o, a, b) for o in (0, 1) for a, b in ((0, 2), (1, 3), (1, 1))] + [(0, 1, 2), (1, 1, 2)]),
    }
    places, at = {}, 0
    for name, group in groups.items():
        places[name] = at
        at += len(group)
    scalars = (jnp.stack([v for group in groups.values() for v in group]).astype(jnp.int32), places)

    own = jnp.concatenate([tokens, hess_tokens], 0)
    z_m, z_p, y_own = send(own, Z_UP), send(own, Z_DOWN), send(own, Y_TWO)
    z_m, z_p, y_own = lax.optimization_barrier((z_m, z_p, y_own))

    y_m, y_p = send(y_own, Z_UP), send(y_own, Z_DOWN)
    z_far = send(jnp.where(core == 0, z_m, z_p), Z_CORE)
    hess_a = jnp.concatenate([r[TOK:] for r in (own, z_m, z_p, y_own)], 0)
    hess_a_other = send(hess_a, Y_PAIR)
    pair = send(jnp.concatenate([columns(probes, False), columns(hess_upstream, False)], 0), Y_PAIR)
    tok_one = jnp.concatenate([r[:TOK] for r in (own, z_m, z_p, y_own)], 0)
    one_toks = [(r, 0, 512) for r in (tok_one, send(tok_one, SWAP))]
    slopes_one = forward(one_toks, weight, upstream, scalars, "one")
    y_m, y_p, z_far, hess_a_other, pair, slopes_one = lax.optimization_barrier(
        (y_m, y_p, z_far, hess_a_other, pair, slopes_one)
    )

    y_far = send(jnp.where(core == 0, y_m, y_p), Z_CORE)
    mine, other = columns(probes, True), pair[:ROWS]
    probe_pair = jnp.concatenate([jnp.where(low, mine, other), jnp.where(low, other, mine)], 0)
    probe_m = send(probe_pair, X_UP)
    probe_p = send(probe_pair, X_DOWN)
    hess_b = jnp.concatenate([r[TOK:] for r in (z_far, y_m, y_p)], 0)
    hess_b_other = send(hess_b, Y_PAIR)
    tok_two = jnp.concatenate([r[:TOK] for r in (after(z_far, probe_pair), y_m, y_p)], 0)
    two_toks = [(r, 0, 384) for r in (tok_two, send(tok_two, SWAP))]
    slopes_two = forward(two_toks, weight, upstream, scalars, "two")
    y_far, slopes_two, hess_b_other = lax.optimization_barrier((y_far, slopes_two, hess_b_other))

    tok_three, hess_c = y_far[:TOK], y_far[TOK:]
    three_toks = [(r, 0, 128) for r in (tok_three, send(tok_three, SWAP))]
    hess_near = jnp.concatenate([hess_a, hess_a_other], 0)
    hess_near_swap = send(hess_near, SWAP)
    hess_c_other = send(hess_c, Y_PAIR)
    probe_2 = send(jnp.where(core == 0, probe_m, probe_p), X_CORE)
    slopes_three = forward(three_toks, weight, upstream, scalars, "three")
    half, whole = slice(0, HALF), slice(0, PAIR)
    def for_other(parts):
        picked = [jnp.where(low, p[:, ROWS:], p[:, :ROWS]).astype(F32) for p in parts]
        return send(sum(picked[1:], picked[0]).astype(BF16), Y_PAIR)

    tok_blocks = one_toks + two_toks + three_toks
    slopes = [slopes_one, slopes_two, slopes_three]
    first, rest = slice(0, 256), slice(256, COLS)
    far_share, far_other, far_own = products(
        tok_blocks,
        slopes,
        scalars,
        0,
        [(512, PAIR)] + [(256, ROWS)] * 2,
        [[(0, 0, rest, whole), (1, 0, first, "other"), (2, 0, first, "own")]],
    )
    far_share = send(far_share, X_CORE)
    far_pair = send(far_other, Y_PAIR)
    hess_b, far_other, probe_2, hess_near_swap = lax.optimization_barrier((hess_b, far_other, probe_2, hess_near_swap))
    hess_rest = jnp.concatenate([hess_b, hess_b_other, hess_c, hess_c_other], 0)
    hess_rest_swap = send(hess_rest, SWAP)
    hess_blocks = [(r, 0, 256) for r in (hess_near, hess_near_swap, hess_rest, hess_rest_swap)]
    probe_parts = [probe_pair, probe_m, probe_p, probe_2]
    hess_values = [
        curved(hess_blocks[:2], weight, probe_parts, [hess_upstream, pair], scalars, "hess near"),
        curved(hess_blocks[2:], weight, probe_parts, [hess_upstream, pair], scalars, "hess rest"),
    ]
    hess_2, hess_up, hess_down, hess_own = products(
        hess_blocks,
        hess_values,
        scalars,
        0,
        [(HALF, PAIR)] * 4,
        [[(g, 0, half, whole)] for g in range(4)],
    )
    order, hess_2 = lax.optimization_barrier((scalars[0], hess_2))
    hess_2 = send(hess_2, X_CORE)
    own, own_other, own_own = products(
        tok_blocks,
        slopes,
        (order, places),
        3,
        [(512, PAIR)] + [(256, ROWS)] * 2,
        [[(0, 0, rest, whole), (1, 0, first, "other"), (2, 0, first, "own")]],
    )
    own_pair = send(own_other, Y_PAIR)
    hess_2, far_share, own = lax.optimization_barrier((hess_2, far_share, own))
    hess_up = plus(hess_up, jnp.where(core == 0, hess_2, 0))
    hess_down = plus(hess_down, jnp.where(core == 0, 0, hess_2))
    order, hess_up, hess_down = lax.optimization_barrier((scalars[0], hess_up, hess_down))
    bends = [hess_own, send(hess_up, X_UP), send(hess_down, X_DOWN)]
    up, down, near_other, near_own = products(
        tok_blocks,
        slopes,
        (order, places),
        1,
        [(512, PAIR)] * 2 + [(512, ROWS)] * 2,
        [[(g, 0, rest, whole), (2, g * 256, first, "other"), (3, g * 256, first, "own")] for g in range(2)],
    )
    near_pair = send(near_other, Y_PAIR)
    bends[1], bends[2], own_pair, up, down = lax.optimization_barrier((bends[1], bends[2], own_pair, up, down))
    up = plus(up, jnp.where(core == 0, far_share, 0))
    down = plus(down, jnp.where(core == 0, 0, far_share))
    late = [own, send(up, X_UP), send(down, X_DOWN)]
    bends.append(for_other(bends))
    new_curvature = curvature_update(scalars, bends, curvature, probes)
    late[1], late[2], far_own, near_own, new_curvature = lax.optimization_barrier(
        (late[1], late[2], far_own, near_own, new_curvature)
    )
    late.append(for_other(late))
    early = [
        send(plus(far_own, far_pair), X_TWO),
        send(plus(near_own[:256], near_pair[:256]), X_UP),
        send(plus(near_own[256:], near_pair[256:]), X_DOWN),
        own_own,
        own_pair,
    ]
    new_weight, new_momentum = update(scalars, late, early, momentum, new_curvature, weight)
    return new_weight, new_momentum, new_curvature


def solution(mesh):
    split = jax.sharding.Mesh(mesh.devices.reshape(SIZES), AXES)
    dp, fsdp = AXES[:2], AXES[2:]
    state = P(dp, fsdp)
    return jax.shard_map(
        shards,
        mesh=split,
        in_specs=(P(AXES, None), P(AXES, None), state, state, P(None, fsdp), state, state, state),
        out_specs=(state, state, state),
        check_vma=False,
    )
```

```python
import math

import jax
import jax.numpy as jnp
from jax import lax
from jax.experimental import pallas as pl
from jax.experimental.pallas import tpu as pltpu
from jax.sharding import PartitionSpec as P

SQRT_HALF = 1.0 / math.sqrt(2.0)
INV_ROOT_TAU = 1.0 / math.sqrt(2.0 * math.pi)
BETA_ONE = 0.965
BETA_TWO = 0.99
LEARN_RATE = 0.0006
WEIGHT_DECAY = 0.1
HESS_SCALE = 0.01
RATIO_FLOOR = 0.001

D = 3072
COLS = 768
HALF = COLS // 2
ROWS = 384
PAIR = 2 * ROWS
TOK = 128
HESS = 32
VMEM = 22 << 20
AXES = ("x", "y_lo", "y_hi", "z", "core")
SIZES = (4, 2, 2, 4, 2)
BF16 = jnp.bfloat16
F32 = jnp.float32


def device_index(x, y, z, core):
    return (x * 2 + y % 2) * 16 + (y // 2) * 8 + z * 2 + core


def moves(step):
    pairs = []
    for x in range(4):
        for y in range(4):
            for z in range(4):
                for core in range(2):
                    if step == "y^":
                        to = (x, y ^ 1, z, core)
                    elif step == "x by core":
                        to = ((x + 1 - 2 * core) % 4, y, z, core)
                    elif step == "z by core":
                        to = (x, y, (z + 1 - 2 * core) % 4, core)
                    else:
                        to = ((x + step[0]) % 4, (y + step[1]) % 4, (z + step[2]) % 4, (core + step[3]) % 2)
                    pairs.append((device_index(x, y, z, core), device_index(*to)))
    return pairs


X_UP, X_DOWN, X_TWO = (1, 0, 0, 0), (3, 0, 0, 0), (2, 0, 0, 0)
Y_UP, Y_DOWN, Y_TWO = (0, 1, 0, 0), (0, 3, 0, 0), (0, 2, 0, 0)
Z_UP, Z_DOWN = (0, 0, 1, 0), (0, 0, 3, 0)
SWAP = (0, 0, 0, 1)
Y_PAIR = "y^"
X_CORE, Z_CORE = "x by core", "z by core"


def send(value, step):
    return lax.ppermute(value, AXES, moves(step))


def gelu_slope(preact):
    normal_cdf = 0.5 * (1.0 + lax.erf(preact * SQRT_HALF))
    density = jnp.exp(-0.5 * preact * preact) * INV_ROOT_TAU
    return normal_cdf + preact * density


def gelu_bend(preact):
    density = jnp.exp(-0.5 * preact * preact) * INV_ROOT_TAU
    return density * (2.0 - preact * preact)


def cost(microseconds):
    return pl.CostEstimate(flops=int(microseconds * 1_000_000_000), bytes_accessed=1000, transcendentals=0)


def after(value, *others):
    return lax.optimization_barrier((value, *others))[0]


ANY = pl.BlockSpec(memory_space=pl.ANY)


class Copies:
    def __init__(self, sems, first=0):
        self.sems, self.next, self.held = sems, first, []

    def start(self, source, target):
        copy = pltpu.make_async_copy(source, target, self.sems.at[self.next])
        copy.start()
        self.next += 1
        self.held.append(copy)

    def wait(self):
        for copy in self.held:
            copy.wait()
        self.held = []


def forward(blocks, weight, upstream, scalars, first):
    first = scalars[1][first]
    n, width, piece = len(blocks), 256, D // 4
    total = sum(rows for _, _, rows in blocks)
    count = total // TOK

    def kernel(first_ref, *refs):
        tokens, w_ref, u_ref, out_ref = refs[:n], refs[n], refs[n + 1], refs[n + 2]
        rows_all, right, signal, sems = refs[n + 3 :]
        some = Copies(sems)

        def fetch(block):
            for k in range(4):
                rows = pl.ds(k * piece, piece)
                some.start(w_ref.at[rows, pl.ds(block * width, width)], right.at[block, rows, :])

        at = 0
        fetch(0)
        for ref, (_, row, rows) in zip(tokens, blocks):
            for j in range(0, rows, TOK):
                some.start(ref.at[pl.ds(row + j, TOK), :], rows_all.at[pl.ds(at + j, TOK), :])
            at += rows
        for j in range(count):
            begin = pl.multiple_of(first_ref[first + j], TOK)
            some.start(u_ref.at[pl.ds(begin, TOK), :], signal.at[pl.ds(j * TOK, TOK), :])
        some.wait()
        for block in range(COLS // width):
            if block + 1 < COLS // width:
                fetch(block + 1)
            cols = slice(block * width, (block + 1) * width)
            for row in range(0, total, 256):
                size = min(256, total - row)
                pre = jnp.dot(rows_all[row : row + size, :], right[block], preferred_element_type=F32)
                value = signal[row : row + size, cols].astype(F32) * gelu_slope(pre)
                out_ref[cols, row : row + size] = value.T.astype(BF16)
            some.wait()

    return pl.pallas_call(
        kernel,
        grid_spec=pltpu.PrefetchScalarGridSpec(
            num_scalar_prefetch=1,
            grid=(1,),
            in_specs=[ANY] * (n + 2),
            out_specs=pl.BlockSpec((COLS, total), lambda i, p: (0, 0)),
            scratch_shapes=[
                pltpu.VMEM((total, D), BF16),
                pltpu.VMEM((COLS // width, D, width), BF16),
                pltpu.VMEM((total, COLS), BF16),
                pltpu.SemaphoreType.DMA((12 + 2 * count,)),
            ],
        ),
        out_shape=jax.ShapeDtypeStruct((COLS, total), BF16),
        compiler_params=pltpu.CompilerParams(vmem_limit_bytes=VMEM),
        cost_estimate=cost(2 + total / 160),
        name="slopes",
    )(scalars[0], *[b for b, _, _ in blocks], weight, upstream)


def curved(blocks, weight, probe_parts, signals, scalars, first):
    n, m = len(blocks), len(probe_parts)
    total = sum(rows for _, _, rows in blocks)
    held = 16 * HESS
    side, starts, first = (scalars[1][name] for name in ("side", "starts", first))

    def kernel(ref_of, *refs):
        rows_refs, w_ref, probe_refs = refs[:n], refs[n], refs[n + 1 : n + 1 + m]
        mine_ref, other_ref, out_ref, right, rows_all, signal, sems = refs[n + 1 + m :]
        some = Copies(sems)
        half = pl.ds(pl.multiple_of(ref_of[side] * HALF, HALF), HALF)
        for k in range(4):
            rows = pl.ds(k * PAIR, PAIR)
            some.start(w_ref.at[rows, half], right.at[rows, pl.ds(0, HALF)])
        for i in range(m):
            rows = pl.ds(pl.multiple_of(ref_of[starts + i], PAIR), PAIR)
            some.start(probe_refs[i], right.at[rows, pl.ds(HALF, HALF)])
        at = 0
        for ref, (_, row, rows) in zip(rows_refs, blocks):
            for j in range(0, rows, 128):
                some.start(ref.at[pl.ds(row + j, 128), :], rows_all.at[pl.ds(at + j, 128), :])
            at += rows
        some.start(mine_ref.at[:, half], signal.at[pl.ds(0, held), :])
        some.start(other_ref.at[pl.ds(ROWS, held), :], signal.at[pl.ds(held, held), :])
        some.wait()
        for row in range(0, total, 256):
            both = jnp.dot(rows_all[row : row + 256, :], right[...], preferred_element_type=F32)
            value = gelu_bend(both[:, :HALF]) * both[:, HALF:]
            signs = []
            for j in range(256 // HESS):
                at = pl.multiple_of(ref_of[first + row // HESS + j], HESS)
                signs.append(signal[pl.ds(at, HESS), :].astype(F32))
            out_ref[:, row : row + 256] = (jnp.concatenate(signs, 0) * value).T.astype(BF16)

    return pl.pallas_call(
        kernel,
        grid_spec=pltpu.PrefetchScalarGridSpec(
            num_scalar_prefetch=1,
            grid=(1,),
            in_specs=[ANY] * (n + 3 + m),
            out_specs=pl.BlockSpec((HALF, total), lambda i, *p: (0, 0)),
            scratch_shapes=[
                pltpu.VMEM((D, COLS), BF16),
                pltpu.VMEM((total, D), BF16),
                pltpu.VMEM((2 * held, HALF), BF16),
                pltpu.SemaphoreType.DMA((6 + m + total // 128,)),
            ],
        ),
        out_shape=jax.ShapeDtypeStruct((HALF, total), BF16),
        compiler_params=pltpu.CompilerParams(vmem_limit_bytes=VMEM),
        cost_estimate=cost(0.1),
        name="curved",
    )(scalars[0], *[b for b, _, _ in blocks], weight, *probe_parts, *signals)


def products(blocks, values, scalars, which, shapes, outs):
    n, m, steps, count = len(blocks), len(values), len(outs), len(shapes)
    total = sum(rows for _, _, rows in blocks)
    height = values[0].shape[0]
    which, side = scalars[1]["targets"] + which, scalars[1]["side"]

    def kernel(ref_of, *refs):
        block_refs, value_refs, out_refs = refs[:n], refs[n : n + m], refs[n + m :]
        left = jnp.concatenate([r[...] for r in value_refs], 1)
        right = jnp.concatenate([r[...] for r in block_refs], 0)
        result = jnp.dot(left, right, preferred_element_type=F32).astype(BF16)
        for k in range(steps):

            @pl.when(pl.program_id(0) == k)
            def _(k=k):
                for out, begin, r, c in outs[k]:
                    if isinstance(c, str):
                        low = (ref_of[side] == 0) == (c == "own")
                        value = jnp.where(low, result[r, :ROWS], result[r, ROWS:])
                    else:
                        value = result[r, c]
                    out_refs[out][begin : begin + r.stop - r.start, :] = value

    return pl.pallas_call(
        kernel,
        grid_spec=pltpu.PrefetchScalarGridSpec(
            num_scalar_prefetch=1,
            grid=(steps,),
            in_specs=[pl.BlockSpec((rows, PAIR), lambda i, p, b=row // rows: (b, p[which + i])) for _, row, rows in blocks]
            + [pl.BlockSpec(v.shape, lambda i, p: (0, 0)) for v in values],
            out_specs=[pl.BlockSpec(s, lambda i, p: (0, 0)) for s in shapes],
        ),
        out_shape=[jax.ShapeDtypeStruct(s, BF16) for s in shapes],
        compiler_params=pltpu.CompilerParams(vmem_limit_bytes=VMEM),
        cost_estimate=cost(0.1 if height == HALF or steps > 1 else 2 + 2.5 * steps),
        name="products",
    )(scalars[0], *[b for b, _, _ in blocks], *values)


def plus(left, right):
    return (left.astype(F32) + right.astype(F32)).astype(BF16)


def share(part, scalars, step):
    side = scalars[1]["side"]
    if part.shape[1] == PAIR:
        return pl.BlockSpec((part.shape[0], step), lambda i, s: (0, s[side] * (ROWS // step) + i))
    return pl.BlockSpec((part.shape[0], step), lambda i, s: (0, i))


def curvature_update(scalars, bends, curvature, probes):
    step, side = 128, scalars[1]["side"]

    def kernel(ref_of, *refs):
        c_ref, p_ref, new_c = refs[len(bends) :]
        values = [ref[...].astype(F32) for ref in refs[: len(bends)]]
        mine, other = sum(values[1:-1], values[0]), values[-1]
        low = ref_of[side] == 0
        bend = jnp.concatenate([jnp.where(low, mine, other), jnp.where(low, other, mine)], 0).T
        new_c[...] = BETA_TWO * c_ref[...] + (1.0 - BETA_TWO) * (p_ref[...].astype(F32) * bend)

    state = pl.BlockSpec((step, COLS), lambda i, s: (i, 0))
    return pl.pallas_call(
        kernel,
        grid_spec=pltpu.PrefetchScalarGridSpec(
            num_scalar_prefetch=1,
            grid=(ROWS // step,),
            in_specs=[share(p, scalars, step) for p in bends] + [state] * 2,
            out_specs=state,
        ),
        out_shape=jax.ShapeDtypeStruct((ROWS, COLS), F32),
        compiler_params=pltpu.CompilerParams(vmem_limit_bytes=VMEM),
        cost_estimate=cost(4),
        name="curvature",
    )(scalars[0], *bends, curvature, probes)


def update(scalars, late, early, momentum, curvature, weight):
    parts = late + early
    split, step, dp = len(late), 128, scalars[1]["dp"]

    def kernel(ref_of, *refs):
        values = [ref[...].astype(F32) for ref in refs[: len(parts)]]
        m_ref, c_ref, w_ref, new_w, new_m = refs[len(parts) :]
        late_sum = sum(values[1:split], values[0])
        early_sum = sum(values[split + 1 :], values[split])
        gradient = jnp.concatenate([early_sum, late_sum], 0).T
        mom = BETA_ONE * m_ref[...] + (1.0 - BETA_ONE) * gradient
        ratio = jnp.clip(mom / jnp.maximum(HESS_SCALE * c_ref[...], RATIO_FLOOR), -1.0, 1.0)
        new_w[...] = (w_ref[...].astype(F32) * (1.0 - LEARN_RATE * WEIGHT_DECAY) - LEARN_RATE * ratio).astype(BF16)
        new_m[...] = mom

    state = pl.BlockSpec((step, COLS), lambda i, s: (i, 0))
    return pl.pallas_call(
        kernel,
        grid_spec=pltpu.PrefetchScalarGridSpec(
            num_scalar_prefetch=1,
            grid=(ROWS // step,),
            in_specs=[share(p, scalars, step) for p in parts]
            + [state] * 2
            + [pl.BlockSpec((step, COLS), lambda i, s: (s[dp] * (ROWS // step) + i, 0))],
            out_specs=[state] * 2,
        ),
        out_shape=[jax.ShapeDtypeStruct((ROWS, COLS), t) for t in (BF16, F32)],
        compiler_params=pltpu.CompilerParams(vmem_limit_bytes=VMEM),
        cost_estimate=cost(4),
        name="update",
    )(scalars[0], *parts, momentum, curvature, weight)


def shards(tokens, hess_tokens, upstream, hess_upstream, weight, probes, momentum, curvature):
    x, y_lo, y_hi, z, core = (lax.axis_index(a) for a in AXES)
    low = y_lo == 0

    def columns(value, own):
        first, last = value[:, :HALF], value[:, HALF:]
        return jnp.where(low, first, last) if own else jnp.where(low, last, first)

    def token_rows(places):
        rows = []
        for step_core, step_y, step_z in places:
            at = ((y_hi + step_y) % 2) * 8 + ((z + step_z) % 4) * 2 + (core + step_core) % 2
            rows.append(TOK * at)
        return rows

    def hess_rows(*groups):
        rows = []
        for group, step_core in [(g, c) for g in groups for c in (0, 1)]:
            for other, step_y, step_z in group:
                place = ((y_hi + step_y) % 2) * 8 + ((z + step_z) % 4) * 2 + (core + step_core) % 2
                rows.append(other * 16 * HESS + place * HESS)
        return rows

    groups = {
        "side": [y_lo],
        "dp": [x * 2 + y_lo],
        "targets": [(x + 2) % 4, (x + 1) % 4, (x + 3) % 4, x],
        "starts": [x * PAIR, (x + 3) % 4 * PAIR, (x + 1) % 4 * PAIR, (x + 2) % 4 * PAIR],
        "one": token_rows([(c, a, b) for c in (0, 1) for a, b in ((0, 0), (0, 3), (0, 1), (1, 0))]),
        "two": token_rows([(c, a, b) for c in (0, 1) for a, b in ((0, 2), (1, 3), (1, 1))]),
        "three": token_rows([(c, 1, 2) for c in (0, 1)]),
        "hess near": hess_rows([(o, a, b) for o in (0, 1) for a, b in ((0, 0), (0, 3), (0, 1), (1, 0))]),
        "hess rest": hess_rows([(o, a, b) for o in (0, 1) for a, b in ((0, 2), (1, 3), (1, 1))] + [(0, 1, 2), (1, 1, 2)]),
    }
    places, at = {}, 0
    for name, group in groups.items():
        places[name] = at
        at += len(group)
    scalars = (jnp.stack([v for group in groups.values() for v in group]).astype(jnp.int32), places)

    own = jnp.concatenate([tokens, hess_tokens], 0)
    z_m, z_p, y_own = send(own, Z_UP), send(own, Z_DOWN), send(own, Y_TWO)
    z_m, z_p, y_own = lax.optimization_barrier((z_m, z_p, y_own))

    y_m, y_p = send(y_own, Z_UP), send(y_own, Z_DOWN)
    z_far = send(jnp.where(core == 0, z_m, z_p), Z_CORE)
    hess_a = jnp.concatenate([r[TOK:] for r in (own, z_m, z_p, y_own)], 0)
    hess_a_other = send(hess_a, Y_PAIR)
    pair = send(jnp.concatenate([columns(probes, False), columns(hess_upstream, False)], 0), Y_PAIR)
    tok_one = jnp.concatenate([r[:TOK] for r in (own, z_m, z_p, y_own)], 0)
    one_toks = [(r, 0, 512) for r in (tok_one, send(tok_one, SWAP))]
    slopes_one = forward(one_toks, weight, upstream, scalars, "one")
    y_m, y_p, z_far, hess_a_other, pair, slopes_one = lax.optimization_barrier(
        (y_m, y_p, z_far, hess_a_other, pair, slopes_one)
    )

    y_far = send(jnp.where(core == 0, y_m, y_p), Z_CORE)
    mine, other = columns(probes, True), pair[:ROWS]
    probe_pair = jnp.concatenate([jnp.where(low, mine, other), jnp.where(low, other, mine)], 0)
    probe_m = send(probe_pair, X_UP)
    probe_p = send(probe_pair, X_DOWN)
    hess_b = jnp.concatenate([r[TOK:] for r in (z_far, y_m, y_p)], 0)
    hess_b_other = send(hess_b, Y_PAIR)
    tok_two = jnp.concatenate([r[:TOK] for r in (after(z_far, probe_pair), y_m, y_p)], 0)
    two_toks = [(r, 0, 384) for r in (tok_two, send(tok_two, SWAP))]
    slopes_two = forward(two_toks, weight, upstream, scalars, "two")
    y_far, slopes_two, hess_b_other = lax.optimization_barrier((y_far, slopes_two, hess_b_other))

    tok_three, hess_c = y_far[:TOK], y_far[TOK:]
    three_toks = [(r, 0, 128) for r in (tok_three, send(tok_three, SWAP))]
    hess_near = jnp.concatenate([hess_a, hess_a_other], 0)
    hess_near_swap = send(hess_near, SWAP)
    hess_c_other = send(hess_c, Y_PAIR)
    probe_2 = send(jnp.where(core == 0, probe_m, probe_p), X_CORE)
    slopes_three = forward(three_toks, weight, upstream, scalars, "three")
    half, whole = slice(0, HALF), slice(0, PAIR)
    def for_other(parts):
        picked = [jnp.where(low, p[:, ROWS:], p[:, :ROWS]).astype(F32) for p in parts]
        return send(sum(picked[1:], picked[0]).astype(BF16), Y_PAIR)

    tok_blocks = one_toks + two_toks + three_toks
    slopes = [slopes_one, slopes_two, slopes_three]
    first, rest = slice(0, 256), slice(256, COLS)
    far_share, far_other, far_own = products(
        tok_blocks,
        slopes,
        scalars,
        0,
        [(512, PAIR)] + [(256, ROWS)] * 2,
        [[(0, 0, rest, whole), (1, 0, first, "other"), (2, 0, first, "own")]],
    )
    far_share = send(far_share, X_CORE)
    far_pair = send(far_other, Y_PAIR)
    hess_b, far_other, probe_2, hess_near_swap = lax.optimization_barrier((hess_b, far_other, probe_2, hess_near_swap))
    hess_rest = jnp.concatenate([hess_b, hess_b_other, hess_c, hess_c_other], 0)
    hess_rest_swap = send(hess_rest, SWAP)
    up, down, near_other, near_own = products(
        tok_blocks,
        slopes,
        (after(scalars[0], far_other), places),
        1,
        [(512, PAIR)] * 2 + [(512, ROWS)] * 2,
        [[(g, 0, rest, whole), (2, g * 256, first, "other"), (3, g * 256, first, "own")] for g in range(2)],
    )
    near_pair = send(near_other, Y_PAIR)
    hess_blocks = [(r, 0, 256) for r in (hess_near, hess_near_swap, hess_rest, hess_rest_swap)]
    probe_parts = [probe_pair, probe_m, probe_p, probe_2]
    signals = [hess_upstream, pair]
    far_share, up, down = lax.optimization_barrier((far_share, up, down))
    up = plus(up, jnp.where(core == 0, far_share, 0))
    down = plus(down, jnp.where(core == 0, 0, far_share))
    order, up, down = lax.optimization_barrier((scalars[0], up, down))
    late = [send(up, X_UP), send(down, X_DOWN)]
    curved_near = curved(hess_blocks[:2], weight, probe_parts, signals, (order, places), "hess near")
    curved_rest = curved(hess_blocks[2:], weight, probe_parts, signals, (order, places), "hess rest")
    hess_2, hess_up, hess_down, hess_own = products(
        hess_blocks,
        [curved_near, curved_rest],
        scalars,
        0,
        [(HALF, PAIR)] * 4,
        [[(g, 0, half, whole)] for g in range(4)],
    )
    order, hess_2 = lax.optimization_barrier((scalars[0], hess_2))
    hess_2 = send(hess_2, X_CORE)
    own, own_other, own_own = products(
        tok_blocks,
        slopes,
        (order, places),
        3,
        [(512, PAIR)] + [(256, ROWS)] * 2,
        [[(0, 0, rest, whole), (1, 0, first, "other"), (2, 0, first, "own")]],
    )
    own_pair = send(own_other, Y_PAIR)
    hess_2, own, own_pair, near_pair, far_pair, *late = lax.optimization_barrier(
        (hess_2, own, own_pair, near_pair, far_pair, *late)
    )
    hess_up = plus(hess_up, jnp.where(core == 0, hess_2, 0))
    hess_down = plus(hess_down, jnp.where(core == 0, 0, hess_2))
    late = [own, *late]
    late.append(for_other(late))
    bends = [hess_own, send(hess_up, X_UP), send(hess_down, X_DOWN)]
    early = [
        send(plus(far_own, far_pair), X_TWO),
        send(plus(near_own[:256], near_pair[:256]), X_UP),
        send(plus(near_own[256:], near_pair[256:]), X_DOWN),
        own_own,
        own_pair,
    ]
    bends.append(for_other(bends))
    order, late[3], *early = lax.optimization_barrier((scalars[0], late[3], *early))
    new_curvature = curvature_update((order, places), bends, curvature, probes)
    new_weight, new_momentum = update(scalars, late, early, momentum, new_curvature, weight)
    return new_weight, new_momentum, new_curvature


def solution(mesh):
    split = jax.sharding.Mesh(mesh.devices.reshape(SIZES), AXES)
    dp, fsdp = AXES[:2], AXES[2:]
    state = P(dp, fsdp)
    return jax.shard_map(
        shards,
        mesh=split,
        in_specs=(P(AXES, None), P(AXES, None), state, state, P(None, fsdp), state, state, state),
        out_specs=(state, state, state),
        check_vma=False,
    )
```

```python
import math

import jax
import jax.numpy as jnp
from jax import lax
from jax.experimental import pallas as pl
from jax.experimental.pallas import tpu as pltpu
from jax.sharding import PartitionSpec as P

SQRT_HALF = 1.0 / math.sqrt(2.0)
INV_ROOT_TAU = 1.0 / math.sqrt(2.0 * math.pi)
BETA_ONE = 0.965
BETA_TWO = 0.99
LEARN_RATE = 0.0006
WEIGHT_DECAY = 0.1
HESS_SCALE = 0.01
RATIO_FLOOR = 0.001

D = 3072
COLS = 768
HALF = COLS // 2
ROWS = 384
PAIR = 2 * ROWS
TOK = 128
HESS = 32
VMEM = 22 << 20
AXES = ("x", "y_lo", "y_hi", "z", "core")
SIZES = (4, 2, 2, 4, 2)
BF16 = jnp.bfloat16
F32 = jnp.float32


def device_index(x, y, z, core):
    return (x * 2 + y % 2) * 16 + (y // 2) * 8 + z * 2 + core


def moves(step):
    pairs = []
    for x in range(4):
        for y in range(4):
            for z in range(4):
                for core in range(2):
                    if step == "y^":
                        to = (x, y ^ 1, z, core)
                    elif step == "x by core":
                        to = ((x + 1 - 2 * core) % 4, y, z, core)
                    elif step == "z by core":
                        to = (x, y, (z + 1 - 2 * core) % 4, core)
                    else:
                        to = ((x + step[0]) % 4, (y + step[1]) % 4, (z + step[2]) % 4, (core + step[3]) % 2)
                    pairs.append((device_index(x, y, z, core), device_index(*to)))
    return pairs


X_UP, X_DOWN, X_TWO = (1, 0, 0, 0), (3, 0, 0, 0), (2, 0, 0, 0)
Y_UP, Y_DOWN, Y_TWO = (0, 1, 0, 0), (0, 3, 0, 0), (0, 2, 0, 0)
Z_UP, Z_DOWN = (0, 0, 1, 0), (0, 0, 3, 0)
SWAP = (0, 0, 0, 1)
Y_PAIR = "y^"
X_CORE, Z_CORE = "x by core", "z by core"


def send(value, step):
    return lax.ppermute(value, AXES, moves(step))


def gelu_slope(preact):
    normal_cdf = 0.5 * (1.0 + lax.erf(preact * SQRT_HALF))
    density = jnp.exp(-0.5 * preact * preact) * INV_ROOT_TAU
    return normal_cdf + preact * density


def gelu_bend(preact):
    density = jnp.exp(-0.5 * preact * preact) * INV_ROOT_TAU
    return density * (2.0 - preact * preact)


def cost(microseconds):
    return pl.CostEstimate(flops=int(microseconds * 1_000_000_000), bytes_accessed=1000, transcendentals=0)


def after(value, *others):
    return lax.optimization_barrier((value, *others))[0]


ANY = pl.BlockSpec(memory_space=pl.ANY)


class Copies:
    def __init__(self, sems, first=0):
        self.sems, self.next, self.held = sems, first, []

    def start(self, source, target):
        copy = pltpu.make_async_copy(source, target, self.sems.at[self.next])
        copy.start()
        self.next += 1
        self.held.append(copy)

    def wait(self):
        for copy in self.held:
            copy.wait()
        self.held = []


def forward(blocks, weight, upstream, scalars, first):
    first = scalars[1][first]
    n, width, piece = len(blocks), 256, D // 4
    total = sum(rows for _, _, rows in blocks)
    count = total // TOK

    def kernel(first_ref, *refs):
        tokens, w_ref, u_ref, out_ref = refs[:n], refs[n], refs[n + 1], refs[n + 2]
        rows_all, right, signal, sems = refs[n + 3 :]
        some = Copies(sems)

        def fetch(block):
            for k in range(4):
                rows = pl.ds(k * piece, piece)
                some.start(w_ref.at[rows, pl.ds(block * width, width)], right.at[block, rows, :])

        at = 0
        fetch(0)
        for ref, (_, row, rows) in zip(tokens, blocks):
            for j in range(0, rows, TOK):
                some.start(ref.at[pl.ds(row + j, TOK), :], rows_all.at[pl.ds(at + j, TOK), :])
            at += rows
        for j in range(count):
            begin = pl.multiple_of(first_ref[first + j], TOK)
            some.start(u_ref.at[pl.ds(begin, TOK), :], signal.at[pl.ds(j * TOK, TOK), :])
        some.wait()
        for block in range(COLS // width):
            if block + 1 < COLS // width:
                fetch(block + 1)
            cols = slice(block * width, (block + 1) * width)
            for row in range(0, total, 256):
                size = min(256, total - row)
                pre = jnp.dot(rows_all[row : row + size, :], right[block], preferred_element_type=F32)
                value = signal[row : row + size, cols].astype(F32) * gelu_slope(pre)
                out_ref[cols, row : row + size] = value.T.astype(BF16)
            some.wait()

    return pl.pallas_call(
        kernel,
        grid_spec=pltpu.PrefetchScalarGridSpec(
            num_scalar_prefetch=1,
            grid=(1,),
            in_specs=[ANY] * (n + 2),
            out_specs=pl.BlockSpec((COLS, total), lambda i, p: (0, 0)),
            scratch_shapes=[
                pltpu.VMEM((total, D), BF16),
                pltpu.VMEM((COLS // width, D, width), BF16),
                pltpu.VMEM((total, COLS), BF16),
                pltpu.SemaphoreType.DMA((12 + 2 * count,)),
            ],
        ),
        out_shape=jax.ShapeDtypeStruct((COLS, total), BF16),
        compiler_params=pltpu.CompilerParams(vmem_limit_bytes=VMEM),
        cost_estimate=cost(2 + total / 160),
        name="slopes",
    )(scalars[0], *[b for b, _, _ in blocks], weight, upstream)


def curved(blocks, weight, probe_parts, signals, scalars, first):
    n, m = len(blocks), len(probe_parts)
    total = sum(rows for _, _, rows in blocks)
    held = 16 * HESS
    side, starts, first = (scalars[1][name] for name in ("side", "starts", first))

    def kernel(ref_of, *refs):
        rows_refs, w_ref, probe_refs = refs[:n], refs[n], refs[n + 1 : n + 1 + m]
        mine_ref, other_ref, out_ref, right, rows_all, signal, sems = refs[n + 1 + m :]
        some = Copies(sems)
        half = pl.ds(pl.multiple_of(ref_of[side] * HALF, HALF), HALF)
        for k in range(4):
            rows = pl.ds(k * PAIR, PAIR)
            some.start(w_ref.at[rows, half], right.at[rows, pl.ds(0, HALF)])
        for i in range(m):
            rows = pl.ds(pl.multiple_of(ref_of[starts + i], PAIR), PAIR)
            some.start(probe_refs[i], right.at[rows, pl.ds(HALF, HALF)])
        at = 0
        for ref, (_, row, rows) in zip(rows_refs, blocks):
            for j in range(0, rows, 128):
                some.start(ref.at[pl.ds(row + j, 128), :], rows_all.at[pl.ds(at + j, 128), :])
            at += rows
        some.start(mine_ref.at[:, half], signal.at[pl.ds(0, held), :])
        some.start(other_ref.at[pl.ds(ROWS, held), :], signal.at[pl.ds(held, held), :])
        some.wait()
        for row in range(0, total, 256):
            both = jnp.dot(rows_all[row : row + 256, :], right[...], preferred_element_type=F32)
            value = gelu_bend(both[:, :HALF]) * both[:, HALF:]
            signs = []
            for j in range(256 // HESS):
                at = pl.multiple_of(ref_of[first + row // HESS + j], HESS)
                signs.append(signal[pl.ds(at, HESS), :].astype(F32))
            out_ref[:, row : row + 256] = (jnp.concatenate(signs, 0) * value).T.astype(BF16)

    return pl.pallas_call(
        kernel,
        grid_spec=pltpu.PrefetchScalarGridSpec(
            num_scalar_prefetch=1,
            grid=(1,),
            in_specs=[ANY] * (n + 3 + m),
            out_specs=pl.BlockSpec((HALF, total), lambda i, *p: (0, 0)),
            scratch_shapes=[
                pltpu.VMEM((D, COLS), BF16),
                pltpu.VMEM((total, D), BF16),
                pltpu.VMEM((2 * held, HALF), BF16),
                pltpu.SemaphoreType.DMA((6 + m + total // 128,)),
            ],
        ),
        out_shape=jax.ShapeDtypeStruct((HALF, total), BF16),
        compiler_params=pltpu.CompilerParams(vmem_limit_bytes=VMEM),
        cost_estimate=cost(0.1),
        name="curved",
    )(scalars[0], *[b for b, _, _ in blocks], weight, *probe_parts, *signals)


def products(blocks, values, scalars, which, shapes, outs):
    n, m, steps, count = len(blocks), len(values), len(outs), len(shapes)
    total = sum(rows for _, _, rows in blocks)
    height = values[0].shape[0]
    which, side = scalars[1]["targets"] + which, scalars[1]["side"]

    def kernel(ref_of, *refs):
        block_refs, value_refs, out_refs = refs[:n], refs[n : n + m], refs[n + m :]
        left = jnp.concatenate([r[...] for r in value_refs], 1)
        right = jnp.concatenate([r[...] for r in block_refs], 0)
        result = jnp.dot(left, right, preferred_element_type=F32).astype(BF16)
        for k in range(steps):

            @pl.when(pl.program_id(0) == k)
            def _(k=k):
                for out, begin, r, c in outs[k]:
                    if isinstance(c, str):
                        low = (ref_of[side] == 0) == (c == "own")
                        value = jnp.where(low, result[r, :ROWS], result[r, ROWS:])
                    else:
                        value = result[r, c]
                    out_refs[out][begin : begin + r.stop - r.start, :] = value

    return pl.pallas_call(
        kernel,
        grid_spec=pltpu.PrefetchScalarGridSpec(
            num_scalar_prefetch=1,
            grid=(steps,),
            in_specs=[pl.BlockSpec((rows, PAIR), lambda i, p, b=row // rows: (b, p[which + i])) for _, row, rows in blocks]
            + [pl.BlockSpec(v.shape, lambda i, p: (0, 0)) for v in values],
            out_specs=[pl.BlockSpec(s, lambda i, p: (0, 0)) for s in shapes],
        ),
        out_shape=[jax.ShapeDtypeStruct(s, BF16) for s in shapes],
        compiler_params=pltpu.CompilerParams(vmem_limit_bytes=VMEM),
        cost_estimate=cost(0.1 if height == HALF or steps > 1 else 2 + 2.5 * steps),
        name="products",
    )(scalars[0], *[b for b, _, _ in blocks], *values)


def plus(left, right):
    return (left.astype(F32) + right.astype(F32)).astype(BF16)


def share(part, scalars, step):
    side = scalars[1]["side"]
    if part.shape[1] == PAIR:
        return pl.BlockSpec((part.shape[0], step), lambda i, s: (0, s[side] * (ROWS // step) + i))
    return pl.BlockSpec((part.shape[0], step), lambda i, s: (0, i))


def curvature_update(scalars, bends, curvature, probes):
    step, side = 128, scalars[1]["side"]

    def kernel(ref_of, *refs):
        c_ref, p_ref, new_c = refs[len(bends) :]
        values = [ref[...].astype(F32) for ref in refs[: len(bends)]]
        mine, other = sum(values[1:-1], values[0]), values[-1]
        low = ref_of[side] == 0
        bend = jnp.concatenate([jnp.where(low, mine, other), jnp.where(low, other, mine)], 0).T
        new_c[...] = BETA_TWO * c_ref[...] + (1.0 - BETA_TWO) * (p_ref[...].astype(F32) * bend)

    state = pl.BlockSpec((step, COLS), lambda i, s: (i, 0))
    return pl.pallas_call(
        kernel,
        grid_spec=pltpu.PrefetchScalarGridSpec(
            num_scalar_prefetch=1,
            grid=(ROWS // step,),
            in_specs=[share(p, scalars, step) for p in bends] + [state] * 2,
            out_specs=state,
        ),
        out_shape=jax.ShapeDtypeStruct((ROWS, COLS), F32),
        compiler_params=pltpu.CompilerParams(vmem_limit_bytes=VMEM),
        cost_estimate=cost(4),
        name="curvature",
    )(scalars[0], *bends, curvature, probes)


def update(scalars, late, early, momentum, curvature, weight):
    parts = late + early
    split, step, dp = len(late), 128, scalars[1]["dp"]

    def kernel(ref_of, *refs):
        values = [ref[...].astype(F32) for ref in refs[: len(parts)]]
        m_ref, c_ref, w_ref, new_w, new_m = refs[len(parts) :]
        late_sum = sum(values[1:split], values[0])
        early_sum = sum(values[split + 1 :], values[split])
        gradient = jnp.concatenate([early_sum, late_sum], 0).T
        mom = BETA_ONE * m_ref[...] + (1.0 - BETA_ONE) * gradient
        ratio = jnp.clip(mom / jnp.maximum(HESS_SCALE * c_ref[...], RATIO_FLOOR), -1.0, 1.0)
        new_w[...] = (w_ref[...].astype(F32) * (1.0 - LEARN_RATE * WEIGHT_DECAY) - LEARN_RATE * ratio).astype(BF16)
        new_m[...] = mom

    state = pl.BlockSpec((step, COLS), lambda i, s: (i, 0))
    return pl.pallas_call(
        kernel,
        grid_spec=pltpu.PrefetchScalarGridSpec(
            num_scalar_prefetch=1,
            grid=(ROWS // step,),
            in_specs=[share(p, scalars, step) for p in parts]
            + [state] * 2
            + [pl.BlockSpec((step, COLS), lambda i, s: (s[dp] * (ROWS // step) + i, 0))],
            out_specs=[state] * 2,
        ),
        out_shape=[jax.ShapeDtypeStruct((ROWS, COLS), t) for t in (BF16, F32)],
        compiler_params=pltpu.CompilerParams(vmem_limit_bytes=VMEM),
        cost_estimate=cost(4),
        name="update",
    )(scalars[0], *parts, momentum, curvature, weight)


def shards(tokens, hess_tokens, upstream, hess_upstream, weight, probes, momentum, curvature):
    x, y_lo, y_hi, z, core = (lax.axis_index(a) for a in AXES)
    low = y_lo == 0

    def columns(value, own):
        first, last = value[:, :HALF], value[:, HALF:]
        return jnp.where(low, first, last) if own else jnp.where(low, last, first)

    def token_rows(places):
        rows = []
        for step_core, step_y, step_z in places:
            at = ((y_hi + step_y) % 2) * 8 + ((z + step_z) % 4) * 2 + (core + step_core) % 2
            rows.append(TOK * at)
        return rows

    def hess_rows(*groups):
        rows = []
        for group, step_core in [(g, c) for g in groups for c in (0, 1)]:
            for other, step_y, step_z in group:
                place = ((y_hi + step_y) % 2) * 8 + ((z + step_z) % 4) * 2 + (core + step_core) % 2
                rows.append(other * 16 * HESS + place * HESS)
        return rows

    groups = {
        "side": [y_lo],
        "dp": [x * 2 + y_lo],
        "targets": [(x + 2) % 4, (x + 1) % 4, (x + 3) % 4, x],
        "starts": [x * PAIR, (x + 3) % 4 * PAIR, (x + 1) % 4 * PAIR, (x + 2) % 4 * PAIR],
        "one": token_rows([(c, a, b) for c in (0, 1) for a, b in ((0, 0), (0, 3), (0, 1), (1, 0))]),
        "two": token_rows([(c, a, b) for c in (0, 1) for a, b in ((0, 2), (1, 3), (1, 1))]),
        "three": token_rows([(c, 1, 2) for c in (0, 1)]),
        "hess near": hess_rows([(o, a, b) for o in (0, 1) for a, b in ((0, 0), (0, 3), (0, 1), (1, 0))]),
        "hess rest": hess_rows([(o, a, b) for o in (0, 1) for a, b in ((0, 2), (1, 3), (1, 1))] + [(0, 1, 2), (1, 1, 2)]),
    }
    places, at = {}, 0
    for name, group in groups.items():
        places[name] = at
        at += len(group)
    scalars = (jnp.stack([v for group in groups.values() for v in group]).astype(jnp.int32), places)

    own = jnp.concatenate([tokens, hess_tokens], 0)
    z_m, z_p, y_own = send(own, Z_UP), send(own, Z_DOWN), send(own, Y_TWO)
    z_m, z_p, y_own = lax.optimization_barrier((z_m, z_p, y_own))

    y_m, y_p = send(y_own, Z_UP), send(y_own, Z_DOWN)
    z_far = send(jnp.where(core == 0, z_m, z_p), Z_CORE)
    hess_a = jnp.concatenate([r[TOK:] for r in (own, z_m, z_p, y_own)], 0)
    hess_a_other = send(hess_a, Y_PAIR)
    pair = send(jnp.concatenate([columns(probes, False), columns(hess_upstream, False)], 0), Y_PAIR)
    tok_one = jnp.concatenate([r[:TOK] for r in (own, z_m, z_p, y_own)], 0)
    one_toks = [(r, 0, 512) for r in (tok_one, send(tok_one, SWAP))]
    slopes_one = forward(one_toks, weight, upstream, scalars, "one")
    y_m, y_p, z_far, hess_a_other, pair, slopes_one = lax.optimization_barrier(
        (y_m, y_p, z_far, hess_a_other, pair, slopes_one)
    )

    y_far = send(jnp.where(core == 0, y_m, y_p), Z_CORE)
    mine, other = columns(probes, True), pair[:ROWS]
    probe_pair = jnp.concatenate([jnp.where(low, mine, other), jnp.where(low, other, mine)], 0)
    probe_m = send(probe_pair, X_UP)
    probe_p = send(probe_pair, X_DOWN)
    hess_b = jnp.concatenate([r[TOK:] for r in (z_far, y_m, y_p)], 0)
    hess_b_other = send(hess_b, Y_PAIR)
    tok_two = jnp.concatenate([r[:TOK] for r in (after(z_far, probe_pair), y_m, y_p)], 0)
    two_toks = [(r, 0, 384) for r in (tok_two, send(tok_two, SWAP))]
    slopes_two = forward(two_toks, weight, upstream, scalars, "two")
    y_far, slopes_two, hess_b_other = lax.optimization_barrier((y_far, slopes_two, hess_b_other))

    tok_three, hess_c = y_far[:TOK], y_far[TOK:]
    three_toks = [(r, 0, 128) for r in (tok_three, send(tok_three, SWAP))]
    hess_near = jnp.concatenate([hess_a, hess_a_other], 0)
    hess_near_swap = send(hess_near, SWAP)
    hess_c_other = send(hess_c, Y_PAIR)
    probe_2 = send(jnp.where(core == 0, probe_m, probe_p), X_CORE)
    slopes_three = forward(three_toks, weight, upstream, scalars, "three")
    half, whole = slice(0, HALF), slice(0, PAIR)
    def for_other(parts):
        picked = [jnp.where(low, p[:, ROWS:], p[:, :ROWS]).astype(F32) for p in parts]
        return send(sum(picked[1:], picked[0]).astype(BF16), Y_PAIR)

    tok_blocks = one_toks + two_toks + three_toks
    slopes = [slopes_one, slopes_two, slopes_three]
    first, rest = slice(0, 256), slice(256, COLS)
    far_share, far_other, far_own = products(
        tok_blocks,
        slopes,
        scalars,
        0,
        [(512, PAIR)] + [(256, ROWS)] * 2,
        [[(0, 0, rest, whole), (1, 0, first, "other"), (2, 0, first, "own")]],
    )
    far_share = send(far_share, X_CORE)
    far_pair = send(far_other, Y_PAIR)
    hess_b, far_other, probe_2, hess_near_swap = lax.optimization_barrier((hess_b, far_other, probe_2, hess_near_swap))
    hess_rest = jnp.concatenate([hess_b, hess_b_other, hess_c, hess_c_other], 0)
    hess_rest_swap = send(hess_rest, SWAP)
    up, down, own, near_other, near_own = products(
        tok_blocks,
        slopes,
        (after(scalars[0], far_other), places),
        1,
        [(512, PAIR)] * 3 + [(768, ROWS)] * 2,
        [[(g, 0, rest, whole), (3, g * 256, first, "other"), (4, g * 256, first, "own")] for g in range(3)],
    )
    near_pair = send(near_other, Y_PAIR)
    hess_blocks = [(r, 0, 256) for r in (hess_near, hess_near_swap, hess_rest, hess_rest_swap)]
    probe_parts = [probe_pair, probe_m, probe_p, probe_2]
    signals = [hess_upstream, pair]
    far_share, up, down = lax.optimization_barrier((far_share, up, down))
    up = plus(up, jnp.where(core == 0, far_share, 0))
    down = plus(down, jnp.where(core == 0, 0, far_share))
    order, up, down = lax.optimization_barrier((scalars[0], up, down))
    late = [send(up, X_UP), send(down, X_DOWN)]
    curved_near = curved(hess_blocks[:2], weight, probe_parts, signals, (order, places), "hess near")
    curved_rest = curved(hess_blocks[2:], weight, probe_parts, signals, (order, places), "hess rest")
    hess_2, hess_up, hess_down, hess_own = products(
        hess_blocks,
        [curved_near, curved_rest],
        scalars,
        0,
        [(HALF, PAIR)] * 4,
        [[(g, 0, half, whole)] for g in range(4)],
    )
    hess_2 = send(hess_2, X_CORE)
    hess_2, near_pair, far_pair, *late = lax.optimization_barrier((hess_2, near_pair, far_pair, *late))
    hess_up = plus(hess_up, jnp.where(core == 0, hess_2, 0))
    hess_down = plus(hess_down, jnp.where(core == 0, 0, hess_2))
    late = [own, *late]
    late.append(for_other(late))
    bends = [hess_own, send(hess_up, X_UP), send(hess_down, X_DOWN)]
    early = [
        send(plus(far_own, far_pair), X_TWO),
        send(plus(near_own[:256], near_pair[:256]), X_UP),
        send(plus(near_own[256:512], near_pair[256:512]), X_DOWN),
        near_own[512:],
        near_pair[512:],
    ]
    bends.append(for_other(bends))
    order, late[3], *early = lax.optimization_barrier((scalars[0], late[3], *early))
    new_curvature = curvature_update((order, places), bends, curvature, probes)
    new_weight, new_momentum = update(scalars, late, early, momentum, new_curvature, weight)
    return new_weight, new_momentum, new_curvature


def solution(mesh):
    split = jax.sharding.Mesh(mesh.devices.reshape(SIZES), AXES)
    dp, fsdp = AXES[:2], AXES[2:]
    state = P(dp, fsdp)
    return jax.shard_map(
        shards,
        mesh=split,
        in_specs=(P(AXES, None), P(AXES, None), state, state, P(None, fsdp), state, state, state),
        out_specs=(state, state, state),
        check_vma=False,
    )
```
